128 devices in a mesh: rep: 4 (over x), row: 32 (over z, y, core).
Axes of the slice: x: 4, y: 4, z: 4, core: 2. Of those that a mesh axis runs over, the one named last changes fastest.
Arguments:
- features: float32 [262144, 128], P(('rep', 'row')), may hold values from -6 to 6
- tile_values: float32 [16384, 128, 128], P(('rep', 'row')), may hold values from -0.25 to 0.25
- tile_owner: int32 [16384, 1], P(('rep', 'row')), may hold values from 0 to 31; in each aligned block of 128 rows (0 to 127, 128 to 255, ...) at most 6 rows name the same one
- tile_local: int32 [16384], P(('rep', 'row')), may hold values from 0 to 15
- tile_source: int32 [16384], P(('rep', 'row')), may hold values from 0 to 63
- w_self: float32 [128, 256], replicated, may hold values from -0.5 to 0.5
- w_neigh: float32 [128, 256], replicated, may hold values from -0.5 to 0.5
- bias: float32 [256], replicated, may hold values from -3 to 3
- cotangent: float32 [262144, 256], P(('rep', 'row')), may hold values from -6 to 6
Outputs:
- output: float32 [262144, 256], P(('rep', 'row'))
- grad_x: float32 [262144, 128], P(('rep', 'row'))
- grad_self: float32 [128, 256], replicated
- grad_neigh: float32 [128, 256], replicated
- grad_bias: float32 [256], replicated
The draws below stay inside these ranges and needn't reach their ends.
Inputs may be any that keep to these rules, and one draw needn't show every extreme that they name: `tile_owner`: among the tiles of one device, no value is named by more than 6 tiles, a bound that some device reaches.
All inputs are finite; a program needn't handle non-finite values.
Results may differ from the reference program's by a relative error of at most 0.0003.
Values sent between devices are 32-bit elements; how exact they have to be, the bound alone decides.
No kernel may reach another device: no remote copies, remote signals or barrier semaphores. Data moves between devices by JAX's collectives and lax.ppermute only.
A program may use at most 128 MiB of HBM per device.

```python
import math
import jax
import jax.numpy as jnp
import numpy as np
from jax import lax

FEAT_IN = 128
HIDDEN_SIZE = 256
BLOCK = 128
BLOCKS_DEV = 16
SLOTS = 6
TILES_DEV = 128
NODES = 262144
TILES = 16384
N_REP = 4
N_ROW = 32
DEVICES = 128


def set_ends(result, key, smallest, high):
    longest = result.shape.index(max(result.shape))
    spots = []
    for shift in (0, 1):
        where = [jax.random.randint(jax.random.fold_in(key, axis), (), 0, length) for axis, length in enumerate(result.shape)]
        where[longest] = (where[longest] + shift) % result.shape[longest]
        spots.append(tuple(where))
    return result.at[spots[0]].set(smallest).at[spots[1]].set(high)


def block_scale(rng, dims, shards, least, top_value):
    def one(position, shards_of):
        steps = jax.random.uniform(jax.random.fold_in(jax.random.fold_in(rng, 6), position), (shards_of,), jnp.float32, least / len(shards), top_value / len(shards))
        return jnp.repeat(jnp.exp(steps), dims[position] // shards_of).reshape((-1,) + (1,) * (len(dims) - position - 1))

    factor_of = one(*shards[0])
    for cut in shards[1:]:
        factor_of = factor_of * one(*cut)
    return factor_of


def deal_out(rng, own, number, rows, number_of, top, limit, slope):
    ranking = jax.random.permutation(rng, number_of)
    heavy_load, common = load_shares(number_of, rows * top, limit, slope, True), load_shares(number_of, rows * top, limit, slope, False)
    places = jnp.arange(number_of)

    def named(sizes, offset_by):
        used = int((sizes > 0).sum())
        fixed = max(1, used // 4)
        moved = fixed + (places - fixed + offset_by * (used - fixed)) % max(1, number_of - fixed)
        return jnp.zeros((number_of,), jnp.int32).at[ranking[jnp.where(places < fixed, places, moved)]].set(jnp.asarray(sizes, jnp.int32))

    sizes = jnp.where(number % 4 == 0, named(heavy_load, number // 4), named(common, number - number // 4 - 1))
    mixed = jax.random.permutation(jax.random.fold_in(own, 3), number_of)
    giver, receiver = mixed[0:number_of // 2 * 2:2], mixed[1:number_of // 2 * 2:2]
    slack = jnp.minimum(sizes[giver] - 1, limit - sizes[receiver]) // 2
    slack = jnp.where((giver == ranking[0]) | (receiver == ranking[0]) | (sizes[receiver] == 0), 0, jnp.maximum(slack, 0))
    moved = jax.random.randint(jax.random.fold_in(own, 4), (number_of // 2,), 0, 1 << 20) % (slack + 1)
    sizes = sizes.at[giver].add(-moved).at[receiver].add(moved)
    items = jnp.searchsorted(jnp.cumsum(sizes), jnp.arange(rows * top), side="right").astype(jnp.int32)
    listing = items.reshape(top, rows).T
    listing = listing[jax.random.permutation(jax.random.fold_in(own, 1), rows)]
    offset_by = jax.random.randint(jax.random.fold_in(own, 2), (rows, 1), 0, top)
    return jnp.take_along_axis(listing, (jnp.arange(top)[None, :] + offset_by) % top, axis=1)


def load_shares(count, total, limit, lean, full):
    weights = [(1 << 20) // math.isqrt(rank ** lean) + 1 for rank in range(1, count + 1)]
    largest = limit if full else min(limit, max(-(-total // count), total * weights[0] // sum(weights)))
    least = 1 if total - largest >= count - 1 else 0
    counts, surplus = [largest] + [least] * (count - 1), total - largest - least * (count - 1)
    while surplus > 0:
        movable = [i for i in range(1, count) if counts[i] < largest] or [i for i in range(1, count) if counts[i] < limit]
        pool, budget = sum([weights[i] for i in movable]), surplus
        for i in movable:
            addition = min(limit - counts[i], max(1, budget * weights[i] // pool), surplus)
            counts[i] = counts[i] + addition
            surplus = surplus - addition
    return np.array(counts)


def centred(own_key, dims, spread, bound, split=(), held_as=jnp.bfloat16):
    drawn = spread * jax.random.normal(own_key, dims, jnp.float32)
    if split:
        drawn = drawn * block_scale(own_key, dims, split, -0.22, 0.18)
    return jnp.clip(drawn, -bound, bound).astype(held_as)


def setup_inputs(seed: int = 0) -> dict:
    streams_of = jax.random.split(jax.random.key(seed), 10)
    features = centred(streams_of[0], (NODES, FEAT_IN), 1.0, 6.0, ((0, 128),), jnp.float32)
    tile_values = centred(streams_of[1], (TILES, BLOCK, BLOCK), (4 * BLOCK) ** -0.5, 0.25, ((0, 128),), jnp.float32)
    tile_owner_keys = jax.random.split(jax.random.fold_in(streams_of[2], 1), TILES // TILES_DEV)
    tile_owner_turns = jax.random.permutation(jax.random.fold_in(streams_of[2], 3), TILES // TILES_DEV)
    tile_owner = jax.vmap(lambda own, number: deal_out(jax.random.fold_in(streams_of[2], 2), own, number, TILES_DEV, N_ROW, 1, SLOTS, 2))(tile_owner_keys, tile_owner_turns).reshape((TILES, 1))
    tile_local = set_ends(jax.random.randint(streams_of[3], (TILES,), 0, BLOCKS_DEV), jax.random.fold_in(streams_of[3], 1), 0, BLOCKS_DEV - 1).astype(jnp.int32)
    tile_source = set_ends(jax.random.randint(streams_of[4], (TILES,), 0, N_REP * BLOCKS_DEV), jax.random.fold_in(streams_of[4], 1), 0, (N_REP * BLOCKS_DEV) - 1).astype(jnp.int32)
    w_self = centred(streams_of[5], (FEAT_IN, HIDDEN_SIZE), FEAT_IN ** -0.5, 0.5, (), jnp.float32)
    w_neigh = centred(streams_of[6], (FEAT_IN, HIDDEN_SIZE), FEAT_IN ** -0.5, 0.5, (), jnp.float32)
    bias = centred(streams_of[7], (HIDDEN_SIZE,), 0.5, 3.0, (), jnp.float32)
    cotangent = centred(streams_of[8], (NODES, HIDDEN_SIZE), 1.0, 6.0, ((0, 128),), jnp.float32)
    return {"features": features, "tile_values": tile_values, "tile_owner": tile_owner, "tile_local": tile_local, "tile_source": tile_source, "w_self": w_self, "w_neigh": w_neigh, "bias": bias, "cotangent": cotangent}


def block_targets(device, owner, local, source):
    rep_index = device // N_ROW
    row_index = device % N_ROW
    dest = (rep_index * N_ROW + owner) * BLOCKS_DEV + local
    src = (source // BLOCKS_DEV * N_ROW + row_index) * BLOCKS_DEV + source % BLOCKS_DEV
    return (dest.astype(jnp.int32), src.astype(jnp.int32))

def reference(features, tile_values, tile_owner, tile_local, tile_source, w_self, w_neigh, bias, cotangent):
    highest = lax.Precision.HIGHEST
    total_blocks = NODES // BLOCK
    node_blocks = features.reshape(total_blocks, BLOCK, FEAT_IN)
    values = tile_values.reshape(DEVICES, TILES_DEV, BLOCK, BLOCK)
    owners = tile_owner.reshape(DEVICES, TILES_DEV)
    locals_all = tile_local.reshape(DEVICES, TILES_DEV)
    sources = tile_source.reshape(DEVICES, TILES_DEV)
    device_ids = jnp.arange(DEVICES, dtype=jnp.int32)

    def forward_step(agg, inputs):
        device, vals, owner, local, source = inputs
        dest, src = block_targets(device, owner, local, source)
        part = jnp.einsum('kij,kjf->kif', vals, node_blocks[src], precision=highest)
        return (agg.at[dest].add(part), None)
    agg_blocks, _ = lax.scan(forward_step, jnp.zeros((total_blocks, BLOCK, FEAT_IN), jnp.float32), (device_ids, values, owners, locals_all, sources))
    aggregated = agg_blocks.reshape(NODES, FEAT_IN)
    pre = jnp.dot(features, w_self, precision=highest, preferred_element_type=jnp.float32) + jnp.dot(aggregated, w_neigh, precision=highest, preferred_element_type=jnp.float32) + bias
    sigma = jax.nn.sigmoid(pre)
    output = pre * sigma
    grad_pre = cotangent * sigma * (1.0 + pre * (1.0 - sigma))
    scale = 1.0 / math.sqrt(NODES)
    grad_self = jnp.dot(features.T, grad_pre, precision=highest, preferred_element_type=jnp.float32) * scale
    grad_neigh = jnp.dot(aggregated.T, grad_pre, precision=highest, preferred_element_type=jnp.float32) * scale
    grad_bias = lax.optimization_barrier(jnp.sum(grad_pre, axis=0)) * scale
    grad_agg = jnp.dot(grad_pre, w_neigh.T, precision=highest, preferred_element_type=jnp.float32)
    agg_grad_blocks = grad_agg.reshape(total_blocks, BLOCK, FEAT_IN)

    def backward_step(acc, inputs):
        device, vals, owner, local, source = inputs
        dest, src = block_targets(device, owner, local, source)
        part = jnp.einsum('kji,kjf->kif', vals, agg_grad_blocks[dest], precision=highest)
        return (acc.at[src].add(part), None)
    source_grads, _ = lax.scan(backward_step, jnp.zeros((total_blocks, BLOCK, FEAT_IN), jnp.float32), (device_ids, values, owners, locals_all, sources))
    grad_x = jnp.dot(grad_pre, w_self.T, precision=highest, preferred_element_type=jnp.float32) + source_grads.reshape(NODES, FEAT_IN)
    return (output, grad_x, grad_self, grad_neigh, grad_bias)
```

```python
import functools
import math

import jax
import jax.numpy as jnp
from jax import lax
from jax.experimental import pallas as pl
from jax.experimental.pallas import tpu as pltpu
from jax.sharding import PartitionSpec as P

SLOTS = 6
BLOCK = 128
FEAT = 128
HID = 256
BLOCKS_DEV = 16
TILES_DEV = 128
N_REP = 4
SIDE = 4
N_ROW = 32
ROW_PARTS = 2
PART = BLOCK // ROW_PARTS
HALF = PART // 2
MSG = 2 * SIDE * SLOTS
DENSE = SIDE * BLOCKS_DEV
ORDER = ((0, 1), (0, 2), (1, 2), (1, 1), (0, 3), (1, 3))
STEP = 8
F32 = jnp.float32
BF16 = jnp.bfloat16
VMEM_LIMIT = 56 * 1024 * 1024

NN = (((1,), (0,)), ((), ()))
NT = (((1,), (1,)), ((), ()))
TN = (((0,), (0,)), ((), ()))


def params():
    return pltpu.CompilerParams(vmem_limit_bytes=VMEM_LIMIT)


def split(x):
    high = x.astype(BF16)
    return high, (x - high.astype(F32)).astype(BF16)


def dot(a, b, dims):
    return lax.dot_general(a, b, dims, preferred_element_type=F32)


def dot3(a, b, dims):
    a_high, a_low = a
    b_high, b_low = b
    return dot(a_high, b_high, dims) + dot(a_low, b_high, dims) + dot(a_high, b_low, dims)


def whole(shape):
    return pl.BlockSpec(shape, lambda *_: (0,) * len(shape))


ANY = pl.BlockSpec(memory_space=pl.ANY)


def forward_kernel(meta, tiles, f0, f1, f2, f3, *rest):
    outs, (slab, send, sems) = rest[: 2 * SIDE], rest[2 * SIDE :]
    step = pl.program_id(0)

    @pl.when(step == 0)
    def _():
        for d, ref in enumerate((f0, f1, f2, f3)):
            high, low = split(ref[...])
            slab[d * BLOCKS_DEV : (d + 1) * BLOCKS_DEV, :, :FEAT] = high
            slab[d * BLOCKS_DEV : (d + 1) * BLOCKS_DEV, :, FEAT:] = low

    for t in range(STEP):
        i = step * STEP + t
        both = dot(jnp.concatenate(split(tiles[t]), axis=0), slab[meta[i]], NN)
        part = both[:PART, :FEAT] + both[PART:, :FEAT] + both[:PART, FEAT:]
        send[meta[TILES_DEV + i]] = part[:HALF]
        send[meta[2 * TILES_DEV + i]] = part[HALF:]

    @pl.when(step == pl.num_programs(0) - 1)
    def _():
        copies = [
            pltpu.make_async_copy(send.at[pl.ds(k * MSG, MSG)], out, sems.at[k])
            for k, out in enumerate(outs)
        ]
        for copy in copies:
            copy.start()
        for copy in copies:
            copy.wait()


def forward_tiles(meta, tile_values, parts, number):
    spec = pltpu.PrefetchScalarGridSpec(
        num_scalar_prefetch=1,
        grid=(TILES_DEV // STEP,),
        in_specs=[pl.BlockSpec((STEP, PART, BLOCK), lambda i, _: (i, number, 0))]
        + [whole((BLOCKS_DEV, BLOCK, FEAT))] * N_REP,
        out_specs=[ANY] * (2 * SIDE),
        scratch_shapes=[
            pltpu.VMEM((N_REP * BLOCKS_DEV, BLOCK, 2 * FEAT), BF16),
            pltpu.VMEM((2 * SIDE * MSG, HALF, FEAT), F32),
            pltpu.SemaphoreType.DMA((2 * SIDE,)),
        ],
    )
    return pl.pallas_call(
        forward_kernel,
        grid_spec=spec,
        out_shape=[jax.ShapeDtypeStruct((MSG, HALF, FEAT), F32)] * (2 * SIDE),
        compiler_params=params(),
        name="forward_tiles",
    )(meta, tile_values, *[p.reshape(BLOCKS_DEV, BLOCK, FEAT) for p in parts])


def combine_kernel(ids, place, *rest):
    received, (keep, give) = rest[: 2 * SIDE], rest[2 * SIDE : 2 * SIDE + 2]
    got, acc, in_sems, sems = rest[-4:]
    z, y, c = place[0], place[1], place[2]
    rows = BLOCKS_DEV + 1
    arrivals = [
        pltpu.make_async_copy(ref, got.at[k], in_sems.at[k]) for k, ref in enumerate(received)
    ]
    for copy in arrivals:
        copy.start()
    acc[...] = jnp.zeros_like(acc)
    copies = []
    for path in range(2):
        for d in range(SIDE):
            if path == 0:
                sender = (z * SIDE + (y + SIDE - d) % SIDE) * 2 + c
            else:
                sender = ((z + SIDE - d) % SIDE * SIDE + y) * 2 + c
            base = sender * (2 * MSG) + path * MSG
            arrivals[path * SIDE + d].wait()
            for s in range(MSG):
                row = (path * 2 * SIDE + s // SLOTS) * rows + ids[base + s]
                acc[row] += got[path * SIDE + d, s]
        for d in range(SIDE):
            target = ((z if path == 0 else y) + d) % SIDE
            for other, out in enumerate((keep, give)):
                copy = pltpu.make_async_copy(
                    acc.at[pl.ds(((path * 2 + other) * SIDE + target) * rows, BLOCKS_DEV)],
                    out.at[pl.ds((path * SIDE + d) * BLOCKS_DEV, BLOCKS_DEV)],
                    sems.at[(path * 2 + other) * SIDE + d],
                )
                copy.start()
                copies.append(copy)
    for copy in copies:
        copy.wait()


def combine(ids, place, received):
    spec = pltpu.PrefetchScalarGridSpec(
        num_scalar_prefetch=2,
        grid=(1,),
        in_specs=[ANY] * (2 * SIDE),
        out_specs=[ANY] * 2,
        scratch_shapes=[
            pltpu.VMEM((2 * SIDE, MSG, HALF, FEAT), F32),
            pltpu.VMEM((4 * SIDE * (BLOCKS_DEV + 1), HALF, FEAT), F32),
            pltpu.SemaphoreType.DMA((2 * SIDE,)),
            pltpu.SemaphoreType.DMA((4 * SIDE,)),
        ],
    )
    return pl.pallas_call(
        combine_kernel,
        grid_spec=spec,
        out_shape=[jax.ShapeDtypeStruct((2 * DENSE, HALF, FEAT), F32)] * 2,
        compiler_params=params(),
        name="combine_blocks",
    )(ids, place, *received)


def add_kernel(keep, taken, *rest):
    outs, (left, right, in_sems, out_sems) = rest[: 2 * SIDE], rest[2 * SIDE :]
    loads, stores = [], []
    for k in range(2 * SIDE):
        rows = pl.ds(k * BLOCKS_DEV, BLOCKS_DEV)
        for n, (ref, buffer) in enumerate(((keep, left), (taken, right))):
            copy = pltpu.make_async_copy(ref.at[rows], buffer.at[k], in_sems.at[2 * k + n])
            copy.start()
            loads.append(copy)
    for k, out in enumerate(outs):
        loads[2 * k].wait()
        loads[2 * k + 1].wait()
        left[k] += right[k]
        copy = pltpu.make_async_copy(left.at[k], out, out_sems.at[k])
        copy.start()
        stores.append(copy)
    for copy in stores:
        copy.wait()


def add_cores(keep, taken):
    return pl.pallas_call(
        add_kernel,
        in_specs=[ANY] * 2,
        out_specs=[ANY] * (2 * SIDE),
        out_shape=[jax.ShapeDtypeStruct((BLOCKS_DEV, HALF, FEAT), F32)] * (2 * SIDE),
        scratch_shapes=[
            pltpu.VMEM((2 * SIDE, BLOCKS_DEV, HALF, FEAT), F32),
            pltpu.VMEM((2 * SIDE, BLOCKS_DEV, HALF, FEAT), F32),
            pltpu.SemaphoreType.DMA((4 * SIDE,)),
            pltpu.SemaphoreType.DMA((2 * SIDE,)),
        ],
        compiler_params=params(),
        name="add_cores",
    )(keep, taken)


PER = 2


def layer_kernel(features, cotangent, w_self, w_neigh, bias, *rest):
    sums, (output, grad_pre, aggregated, grads) = rest[:-4], rest[-4:]
    halves = []
    for b in range(PER):
        for piece in range(2 * ROW_PARTS):
            refs = sums[piece * SIDE : (piece + 1) * SIDE]
            halves.append((refs[0][b] + refs[1][b]) + (refs[2][b] + refs[3][b]))
    agg = jnp.concatenate(halves, axis=0)
    aggregated[...] = agg
    w_neigh_split = split(w_neigh[...])
    pre = (
        dot3(split(features[...]), split(w_self[...]), NN)
        + dot3(split(agg), w_neigh_split, NN)
        + bias[...]
    )
    sigma = jax.nn.sigmoid(pre)
    output[...] = pre * sigma
    grad = cotangent[...] * sigma * (1.0 + pre * (1.0 - sigma))
    grad_pre[...] = grad
    high, low = split(grad)
    for b in range(PER):
        rows = slice(b * BLOCK, (b + 1) * BLOCK)
        grads[b] = dot3(w_neigh_split, (high[rows], low[rows]), NT)


def layer(features, cotangent, w_self, w_neigh, bias, sums):
    nodes = features.shape[0]
    row = lambda width: pl.BlockSpec((PER * BLOCK, width), lambda i: (i, 0))
    block = lambda depth: pl.BlockSpec((PER, depth, BLOCK), lambda i: (i, 0, 0))
    return pl.pallas_call(
        layer_kernel,
        grid=(BLOCKS_DEV // PER,),
        in_specs=[row(FEAT), row(HID), whole((FEAT, HID)), whole((FEAT, HID)), whole((1, HID))]
        + [block(HALF)] * (2 * ROW_PARTS * SIDE),
        out_specs=[row(HID), row(HID), row(FEAT), block(FEAT)],
        out_shape=[
            jax.ShapeDtypeStruct((nodes, HID), F32),
            jax.ShapeDtypeStruct((nodes, HID), F32),
            jax.ShapeDtypeStruct((nodes, FEAT), F32),
            jax.ShapeDtypeStruct((BLOCKS_DEV, FEAT, BLOCK), F32),
        ],
        compiler_params=params(),
        name="layer",
    )(features, cotangent, w_self, w_neigh, bias, *sums)


TERM_ROWS = 2 * FEAT // N_ROW


def terms_kernel(features, aggregated, grad_pre, w_self, own, terms, acc, acc_bias):
    step = pl.program_id(0)

    @pl.when(step == 0)
    def _():
        acc[...] = jnp.zeros_like(acc)
        acc_bias[...] = jnp.zeros_like(acc_bias)

    grad = grad_pre[...]
    parts = split(grad)
    own[...] = dot3(parts, split(w_self[...]), NT)
    acc[:FEAT] += dot3(split(features[...]), parts, TN)
    acc[FEAT:] += dot3(split(aggregated[...]), parts, TN)
    acc_bias[...] += jnp.sum(grad.reshape(-1, 8, HID), axis=0)

    @pl.when(step == pl.num_programs(0) - 1)
    def _():
        total = jnp.sum(acc_bias[...], axis=0, keepdims=True)
        for r in range(N_ROW):
            terms[r, :, :HID] = acc[r * TERM_ROWS : (r + 1) * TERM_ROWS]
            terms[r, :, HID:] = jnp.concatenate(
                [jnp.broadcast_to(total[:, :128], (4, 128)), jnp.broadcast_to(total[:, 128:], (4, 128))],
                axis=0,
            )


def weight_terms(features, aggregated, grad_pre, w_self):
    nodes = features.shape[0]
    row = lambda width: pl.BlockSpec((PER * BLOCK, width), lambda i: (i, 0))
    return pl.pallas_call(
        terms_kernel,
        grid=(BLOCKS_DEV // PER,),
        in_specs=[row(FEAT), row(FEAT), row(HID), whole((FEAT, HID))],
        out_specs=[row(FEAT), whole((N_ROW, TERM_ROWS, HID + 128))],
        out_shape=[
            jax.ShapeDtypeStruct((nodes, FEAT), F32),
            jax.ShapeDtypeStruct((N_ROW, TERM_ROWS, HID + 128), F32),
        ],
        scratch_shapes=[pltpu.VMEM((2 * FEAT, HID), F32), pltpu.VMEM((8, HID), F32)],
        compiler_params=params(),
        name="weight_terms",
    )(features, aggregated, grad_pre, w_self)


def backward_kernel(meta, tiles, grads, *rest):
    outs, (got, acc, sems, out_sems) = rest[:N_REP], rest[N_REP:]
    step = pl.program_id(0)
    steps = pl.num_programs(0)

    @pl.when(step == 0)
    def _():
        def fetch(i, _):
            pltpu.make_async_copy(
                grads.at[meta[TILES_DEV + i]], got.at[i // STEP, i % STEP], sems.at[i // STEP]
            ).start()
            return 0

        lax.fori_loop(0, TILES_DEV, fetch, 0)
        acc[...] = jnp.zeros_like(acc)

    pltpu.make_async_copy(grads.at[pl.ds(0, STEP)], got.at[step], sems.at[step]).wait()
    for t in range(STEP):
        grad = jnp.concatenate(split(got[step, t]), axis=0)
        both = dot(grad, jnp.concatenate(split(tiles[t]), axis=1), NN)
        part = both[:FEAT, :BLOCK] + both[FEAT:, :BLOCK] + both[:FEAT, BLOCK:]
        acc[meta[step * STEP + t]] += part

    @pl.when(step == steps - 1)
    def _():
        rep = meta[2 * TILES_DEV]
        copies = [
            pltpu.make_async_copy(
                acc.at[pl.ds((rep + d) % N_REP * BLOCKS_DEV, BLOCKS_DEV)], out, out_sems.at[d]
            )
            for d, out in enumerate(outs)
        ]
        for copy in copies:
            copy.start()
        for copy in copies:
            copy.wait()


def backward_tiles(meta, tile_values, grads):
    spec = pltpu.PrefetchScalarGridSpec(
        num_scalar_prefetch=1,
        grid=(TILES_DEV // STEP,),
        in_specs=[pl.BlockSpec((STEP, BLOCK, BLOCK), lambda i, _: (i, 0, 0)), ANY],
        out_specs=[ANY] * N_REP,
        scratch_shapes=[
            pltpu.VMEM((TILES_DEV // STEP, STEP, FEAT, BLOCK), F32),
            pltpu.VMEM((N_REP * BLOCKS_DEV, FEAT, BLOCK), F32),
            pltpu.SemaphoreType.DMA((TILES_DEV // STEP,)),
            pltpu.SemaphoreType.DMA((N_REP,)),
        ],
    )
    return pl.pallas_call(
        backward_kernel,
        grid_spec=spec,
        out_shape=[jax.ShapeDtypeStruct((BLOCKS_DEV, FEAT, BLOCK), F32)] * N_REP,
        compiler_params=params(),
        name="backward_tiles",
    )(meta, tile_values, grads)


def finish_kernel(own, *rest):
    sums, out = rest[:-1], rest[-1]
    for b in range(PER):
        total = (sums[0][b] + sums[1][b]) + (sums[2][b] + sums[3][b])
        rows = slice(b * BLOCK, (b + 1) * BLOCK)
        out[rows, :] = own[rows, :] + total.T


def finish(own, sums):
    row = pl.BlockSpec((PER * BLOCK, FEAT), lambda i: (i, 0))
    return pl.pallas_call(
        finish_kernel,
        grid=(BLOCKS_DEV // PER,),
        in_specs=[row] + [pl.BlockSpec((PER, FEAT, BLOCK), lambda i: (i, 0, 0))] * N_REP,
        out_specs=row,
        out_shape=jax.ShapeDtypeStruct(own.shape, F32),
        compiler_params=params(),
        name="finish_grad_x",
    )(own, *sums)


def row_index(z, y, c):
    return (z % SIDE * SIDE + y % SIDE) * 2 + c % 2


def shift(x, dz, dy, dc=0):
    pairs = [
        (row_index(z, y, c), row_index(z + dz, y + dy, c + dc))
        for z in range(SIDE)
        for y in range(SIDE)
        for c in range(2)
    ]
    return lax.ppermute(x, "row", pairs)


def shift_rep(x, d):
    return x if d == 0 else lax.ppermute(x, "rep", [(i, (i + d) % N_REP) for i in range(N_REP)])


def local(
    features, tile_values, tile_owner, tile_local, tile_source, w_self, w_neigh, bias, cotangent
):
    rep, row = lax.axis_index("rep"), lax.axis_index("row")
    z, y, c = row // (2 * SIDE), row // 2 % SIDE, row % 2

    owner = tile_owner[:, 0]
    owner_hot = owner[:, None] == jnp.arange(N_ROW, dtype=jnp.int32)[None, :]
    same = owner[:, None] == owner[None, :]
    earlier = jnp.arange(TILES_DEV)[:, None] > jnp.arange(TILES_DEV)[None, :]
    rank = jnp.sum((same & earlier).astype(jnp.int32), axis=1)
    slot = owner * SLOTS + rank
    o_z, o_y, o_c = owner // (2 * SIDE), owner // 2 % SIDE, owner % 2
    o_core = (o_c - c) % 2
    pos_y = (o_y - y) % SIDE * MSG + (o_core * SIDE + o_z) * SLOTS + rank
    pos_z = ((o_z - z) % SIDE + SIDE) * MSG + (o_core * SIDE + o_y) * SLOTS + rank
    src_rep, src_block = tile_source // BLOCKS_DEV, tile_source % BLOCKS_DEV
    src = (rep - src_rep) % N_REP * BLOCKS_DEV + src_block
    forward_meta = jnp.concatenate([src, pos_y, pos_z]).astype(jnp.int32)
    backward_meta = jnp.concatenate(
        [tile_source, owner * BLOCKS_DEV + tile_local, rep[None]]
    ).astype(jnp.int32)
    place = jnp.stack([z, y, c]).astype(jnp.int32)

    hit = slot[None, :] == jnp.arange(N_ROW * SLOTS, dtype=jnp.int32)[:, None]
    named = jnp.sum(jnp.where(hit, (tile_local - BLOCKS_DEV)[None, :], 0), axis=1) + BLOCKS_DEV
    named = named.reshape(SIDE, SIDE, 2, SLOTS)
    both = jnp.stack([named, named[:, :, ::-1]], axis=3)
    grid = (SIDE, SIDE, 2, 2, SIDE, SLOTS)
    along_z = jnp.broadcast_to(both.transpose(1, 2, 3, 0, 4)[None], grid)
    along_y = jnp.broadcast_to(both.transpose(0, 2, 3, 1, 4)[:, None], grid)
    to_send = jnp.concatenate(
        [along_z.reshape(N_ROW, MSG), along_y.reshape(N_ROW, MSG)], axis=1
    ).astype(jnp.int32)
    ids = lax.all_to_all(to_send, "row", split_axis=0, concat_axis=0, tiled=True).reshape(-1)

    forward_meta, ids = lax.optimization_barrier((forward_meta, ids))
    parts = [features] + [shift_rep(features, d) for d in (1, 2, 3)]
    sums = []
    for number in range(ROW_PARTS):
        got = list(forward_tiles(forward_meta, tile_values, parts, number))
        for path, d in ORDER:
            k = path * SIDE + d
            got[k] = shift(got[k], 0, d) if path == 0 else shift(got[k], d, 0)
        keep, give = combine(ids, place, got)
        dense = list(add_cores(keep, shift(give, 0, 0, 1)))
        for path, d in ORDER:
            k = path * SIDE + d
            dense[k] = shift(dense[k], d, 0) if path == 0 else shift(dense[k], 0, d)
        sums.extend(dense)

    output, grad_pre, aggregated, grads = layer(
        features, cotangent, w_self, w_neigh, bias[None, :], sums
    )

    own, terms = weight_terms(features, aggregated, grad_pre, w_self)
    dealt = lax.all_to_all(terms, "row", split_axis=0, concat_axis=0, tiled=True)
    mine = lax.psum(jnp.sum(dealt, axis=0), "rep")
    full = lax.all_gather(mine, "row", axis=0, tiled=True)
    scale = 1.0 / math.sqrt(features.shape[0] * N_REP * N_ROW)
    grad_self = full[:FEAT, :HID] * scale
    grad_neigh = full[FEAT:, :HID] * scale
    grad_bias = jnp.concatenate([full[0, HID:], full[4, HID:]]) * scale

    gathered = lax.all_gather(grads, "row", axis=0, tiled=True)
    backward_meta, grad_self, grad_neigh, grad_bias = lax.optimization_barrier(
        (backward_meta, grad_self, grad_neigh, grad_bias)
    )
    slab = backward_tiles(backward_meta, tile_values, gathered)
    back = [slab[0]] + [shift_rep(slab[d], d) for d in (1, 2, 3)]
    grad_x = finish(own, back)
    return (output, grad_x, grad_self, grad_neigh, grad_bias)


def solution(mesh):
    return jax.shard_map(
        local,
        mesh=mesh,
        in_specs=(
            P(("rep", "row"), None),
            P(("rep", "row"), None, None),
            P(("rep", "row"), None),
            P(("rep", "row")),
            P(("rep", "row")),
            P(),
            P(),
            P(),
            P(("rep", "row"), None),
        ),
        out_specs=(P(("rep", "row"), None), P(("rep", "row"), None), P(), P(), P()),
        check_vma=False,
    )
```

```python
import functools
import math

import jax
import jax.numpy as jnp
from jax import lax
from jax.experimental import pallas as pl
from jax.experimental.pallas import tpu as pltpu
from jax.sharding import PartitionSpec as P

SLOTS = 6
BLOCK = 128
FEAT = 128
HID = 256
BLOCKS_DEV = 16
TILES_DEV = 128
N_REP = 4
SIDE = 4
N_ROW = 32
SUMMED = 48
HALF = (BLOCK - SUMMED) // 2
MSG = 2 * SIDE * SLOTS
DENSE = SIDE * BLOCKS_DEV
GATHERED = 80
REPLIED = FEAT - GATHERED
REPLY = REPLIED // 2
ORDER = ((0, 1), (0, 2), (1, 2), (1, 1), (0, 3), (1, 3))
STEP = 32
F32 = jnp.float32
BF16 = jnp.bfloat16
VMEM_LIMIT = 56 * 1024 * 1024

NN = (((1,), (0,)), ((), ()))
NT = (((1,), (1,)), ((), ()))
TN = (((0,), (0,)), ((), ()))


def params():
    return pltpu.CompilerParams(vmem_limit_bytes=VMEM_LIMIT)


def split(x):
    high = x.astype(BF16)
    return high, (x - high.astype(F32)).astype(BF16)


def dot(a, b, dims):
    return lax.dot_general(a, b, dims, preferred_element_type=F32)


def dot3(a, b, dims):
    a_high, a_low = a
    b_high, b_low = b
    return dot(a_high, b_high, dims) + dot(a_low, b_high, dims) + dot(a_high, b_low, dims)


def whole(shape):
    return pl.BlockSpec(shape, lambda *_: (0,) * len(shape))


ANY = pl.BlockSpec(memory_space=pl.ANY)


SOURCES = 7


def fill_slab(slab, refs):
    first = 0
    for ref in refs:
        high, low = split(ref[...])
        slab[first : first + ref.shape[0], :, :FEAT] = high
        slab[first : first + ref.shape[0], :, FEAT:] = low
        first += ref.shape[0]


def forward_product(tile, source):
    rows = tile.shape[0]
    both = dot(jnp.concatenate(split(tile), axis=0), source, NN)
    return both[:rows, :FEAT] + both[rows:, :FEAT] + both[:rows, FEAT:]


def forward_kernel(meta, tiles, *rest):
    sources, outs = rest[:SOURCES], rest[SOURCES : SOURCES + 2 * SIDE + 1]
    slab, send, acc, sems = rest[SOURCES + 2 * SIDE + 1 :]
    step = pl.program_id(0)

    @pl.when(step == 0)
    def _():
        fill_slab(slab, sources)
        acc[...] = jnp.zeros_like(acc)

    for t in range(STEP):
        i = step * STEP + t
        part = forward_product(tiles[t], slab[meta[i]])
        send[meta[TILES_DEV + i]] = part[:HALF]
        send[meta[2 * TILES_DEV + i]] = part[HALF : 2 * HALF]
        acc[meta[3 * TILES_DEV + i]] += part[2 * HALF :]

    @pl.when(step == pl.num_programs(0) - 1)
    def _():
        copies = [
            pltpu.make_async_copy(send.at[pl.ds(k * MSG, MSG)], out, sems.at[k])
            for k, out in enumerate(outs[:-1])
        ]
        copies.append(pltpu.make_async_copy(acc, outs[-1], sems.at[2 * SIDE]))
        for copy in copies:
            copy.start()
        for copy in copies:
            copy.wait()


def forward_tiles(meta, tile_values, sources):
    blocks = N_ROW * BLOCKS_DEV
    sources = [x.reshape(-1, BLOCK, FEAT) for x in sources]
    spec = pltpu.PrefetchScalarGridSpec(
        num_scalar_prefetch=1,
        grid=(TILES_DEV // STEP,),
        in_specs=[pl.BlockSpec((STEP, BLOCK, BLOCK), lambda i, _: (i, 0, 0))]
        + [whole(x.shape) for x in sources],
        out_specs=[ANY] * (2 * SIDE + 1),
        scratch_shapes=[
            pltpu.VMEM((N_REP * BLOCKS_DEV, BLOCK, 2 * FEAT), BF16),
            pltpu.VMEM((2 * SIDE * MSG, HALF, FEAT), F32),
            pltpu.VMEM((blocks, SUMMED, FEAT), F32),
            pltpu.SemaphoreType.DMA((2 * SIDE + 1,)),
        ],
    )
    return pl.pallas_call(
        forward_kernel,
        grid_spec=spec,
        out_shape=[jax.ShapeDtypeStruct((MSG, HALF, FEAT), F32)] * (2 * SIDE)
        + [jax.ShapeDtypeStruct((blocks, SUMMED, FEAT), F32)],
        compiler_params=params(),
        name="forward_tiles",
    )(meta, tile_values, *sources)


def combine_kernel(ids, place, *rest):
    received, (keep, give) = rest[: 2 * SIDE], rest[2 * SIDE : 2 * SIDE + 2]
    got, acc, in_sems, sems = rest[-4:]
    z, y, c = place[0], place[1], place[2]
    rows = BLOCKS_DEV + 1
    arrivals = [
        pltpu.make_async_copy(ref, got.at[k], in_sems.at[k]) for k, ref in enumerate(received)
    ]
    for copy in arrivals:
        copy.start()
    acc[...] = jnp.zeros_like(acc)
    copies = []
    for path in range(2):
        for d in range(SIDE):
            if path == 0:
                sender = (z * SIDE + (y + SIDE - d) % SIDE) * 2 + c
            else:
                sender = ((z + SIDE - d) % SIDE * SIDE + y) * 2 + c
            base = sender * (2 * MSG) + path * MSG
            arrivals[path * SIDE + d].wait()
            for s in range(MSG):
                row = (path * 2 * SIDE + s // SLOTS) * rows + ids[base + s]
                acc[row] += got[path * SIDE + d, s]
        for d in range(SIDE):
            target = ((z if path == 0 else y) + d) % SIDE
            for other, out in enumerate((keep, give)):
                copy = pltpu.make_async_copy(
                    acc.at[pl.ds(((path * 2 + other) * SIDE + target) * rows, BLOCKS_DEV)],
                    out.at[pl.ds((path * SIDE + d) * BLOCKS_DEV, BLOCKS_DEV)],
                    sems.at[(path * 2 + other) * SIDE + d],
                )
                copy.start()
                copies.append(copy)
    for copy in copies:
        copy.wait()


def combine(ids, place, received):
    spec = pltpu.PrefetchScalarGridSpec(
        num_scalar_prefetch=2,
        grid=(1,),
        in_specs=[ANY] * (2 * SIDE),
        out_specs=[ANY] * 2,
        scratch_shapes=[
            pltpu.VMEM((2 * SIDE, MSG, HALF, FEAT), F32),
            pltpu.VMEM((4 * SIDE * (BLOCKS_DEV + 1), HALF, FEAT), F32),
            pltpu.SemaphoreType.DMA((2 * SIDE,)),
            pltpu.SemaphoreType.DMA((4 * SIDE,)),
        ],
    )
    return pl.pallas_call(
        combine_kernel,
        grid_spec=spec,
        out_shape=[jax.ShapeDtypeStruct((2 * DENSE, HALF, FEAT), F32)] * 2,
        compiler_params=params(),
        name="combine_blocks",
    )(ids, place, *received)


def add_kernel(keep, taken, *rest):
    outs, (left, right, in_sems, out_sems) = rest[: 2 * SIDE], rest[2 * SIDE :]
    loads, stores = [], []
    for k in range(2 * SIDE):
        rows = pl.ds(k * BLOCKS_DEV, BLOCKS_DEV)
        for n, (ref, buffer) in enumerate(((keep, left), (taken, right))):
            copy = pltpu.make_async_copy(ref.at[rows], buffer.at[k], in_sems.at[2 * k + n])
            copy.start()
            loads.append(copy)
    for k, out in enumerate(outs):
        loads[2 * k].wait()
        loads[2 * k + 1].wait()
        left[k] += right[k]
        copy = pltpu.make_async_copy(left.at[k], out, out_sems.at[k])
        copy.start()
        stores.append(copy)
    for copy in stores:
        copy.wait()


def add_cores(keep, taken):
    return pl.pallas_call(
        add_kernel,
        in_specs=[ANY] * 2,
        out_specs=[ANY] * (2 * SIDE),
        out_shape=[jax.ShapeDtypeStruct((BLOCKS_DEV, HALF, FEAT), F32)] * (2 * SIDE),
        scratch_shapes=[
            pltpu.VMEM((2 * SIDE, BLOCKS_DEV, HALF, FEAT), F32),
            pltpu.VMEM((2 * SIDE, BLOCKS_DEV, HALF, FEAT), F32),
            pltpu.SemaphoreType.DMA((4 * SIDE,)),
            pltpu.SemaphoreType.DMA((2 * SIDE,)),
        ],
        compiler_params=params(),
        name="add_cores",
    )(keep, taken)


PER = 4


def layer_kernel(features, cotangent, w_self, w_neigh, bias, *rest):
    sums, (output, grad_pre, aggregated, gathered, first, second) = rest[:-6], rest[-6:]
    halves = []
    for b in range(PER):
        for piece in range(2):
            refs = sums[piece * SIDE : (piece + 1) * SIDE]
            halves.append((refs[0][b] + refs[1][b]) + (refs[2][b] + refs[3][b]))
        halves.append(sums[-1][b])
    agg = jnp.concatenate(halves, axis=0)
    aggregated[...] = agg
    w_neigh_split = split(w_neigh[...])
    pre = (
        dot3(split(features[...]), split(w_self[...]), NN)
        + dot3(split(agg), w_neigh_split, NN)
        + bias[...]
    )
    sigma = jax.nn.sigmoid(pre)
    output[...] = pre * sigma
    grad = cotangent[...] * sigma * (1.0 + pre * (1.0 - sigma))
    grad_pre[...] = grad
    high, low = split(grad)
    for b in range(PER):
        rows = slice(b * BLOCK, (b + 1) * BLOCK)
        turned = dot3(w_neigh_split, (high[rows], low[rows]), NT)
        gathered[b] = turned[:GATHERED]
        first[b] = turned[GATHERED : GATHERED + REPLY]
        second[b] = turned[GATHERED + REPLY :]


def layer(features, cotangent, w_self, w_neigh, bias, sums):
    nodes = features.shape[0]
    row = lambda width: pl.BlockSpec((PER * BLOCK, width), lambda i: (i, 0))
    block = lambda depth: pl.BlockSpec((PER, depth, BLOCK), lambda i: (i, 0, 0))
    return pl.pallas_call(
        layer_kernel,
        grid=(BLOCKS_DEV // PER,),
        in_specs=[row(FEAT), row(HID), whole((FEAT, HID)), whole((FEAT, HID)), whole((1, HID))]
        + [block(HALF)] * (2 * SIDE)
        + [block(SUMMED)],
        out_specs=[row(HID), row(HID), row(FEAT), block(GATHERED), block(REPLY), block(REPLY)],
        out_shape=[
            jax.ShapeDtypeStruct((nodes, HID), F32),
            jax.ShapeDtypeStruct((nodes, HID), F32),
            jax.ShapeDtypeStruct((nodes, FEAT), F32),
            jax.ShapeDtypeStruct((BLOCKS_DEV, GATHERED, BLOCK), F32),
            jax.ShapeDtypeStruct((BLOCKS_DEV, REPLY, BLOCK), F32),
            jax.ShapeDtypeStruct((BLOCKS_DEV, REPLY, BLOCK), F32),
        ],
        compiler_params=params(),
        name="layer",
    )(features, cotangent, w_self, w_neigh, bias, *sums)


TERM_ROWS = 2 * FEAT // N_ROW


def terms_kernel(features, aggregated, grad_pre, w_self, own, terms, acc, acc_bias):
    step = pl.program_id(0)

    @pl.when(step == 0)
    def _():
        acc[...] = jnp.zeros_like(acc)
        acc_bias[...] = jnp.zeros_like(acc_bias)

    grad = grad_pre[...]
    parts = split(grad)
    own[...] = dot3(parts, split(w_self[...]), NT)
    acc[:FEAT] += dot3(split(features[...]), parts, TN)
    acc[FEAT:] += dot3(split(aggregated[...]), parts, TN)
    acc_bias[...] += jnp.sum(grad.reshape(-1, 8, HID), axis=0)

    @pl.when(step == pl.num_programs(0) - 1)
    def _():
        total = jnp.sum(acc_bias[...], axis=0, keepdims=True)
        for r in range(N_ROW):
            terms[r, :, :HID] = acc[r * TERM_ROWS : (r + 1) * TERM_ROWS]
            terms[r, :, HID:] = jnp.concatenate(
                [jnp.broadcast_to(total[:, :128], (4, 128)), jnp.broadcast_to(total[:, 128:], (4, 128))],
                axis=0,
            )


def weight_terms(features, aggregated, grad_pre, w_self):
    nodes = features.shape[0]
    row = lambda width: pl.BlockSpec((PER * BLOCK, width), lambda i: (i, 0))
    return pl.pallas_call(
        terms_kernel,
        grid=(BLOCKS_DEV // PER,),
        in_specs=[row(FEAT), row(FEAT), row(HID), whole((FEAT, HID))],
        out_specs=[row(FEAT), whole((N_ROW, TERM_ROWS, HID + 128))],
        out_shape=[
            jax.ShapeDtypeStruct((nodes, FEAT), F32),
            jax.ShapeDtypeStruct((N_ROW, TERM_ROWS, HID + 128), F32),
        ],
        scratch_shapes=[pltpu.VMEM((2 * FEAT, HID), F32), pltpu.VMEM((8, HID), F32)],
        compiler_params=params(),
        name="weight_terms",
    )(features, aggregated, grad_pre, w_self)


def reply_kernel(ids, place, mine, taken, *rest):
    outs, (dense, reply, in_sems, out_sems) = rest[: 2 * SIDE], rest[2 * SIDE :]
    z, y, c = place[0], place[1], place[2]
    loads = []
    for n, ref in enumerate((mine, taken)):
        copy = pltpu.make_async_copy(ref, dense.at[n], in_sems.at[n])
        copy.start()
        loads.append(copy)
    for copy in loads:
        copy.wait()
    stores = []
    for path in range(2):
        for d in range(SIDE):
            if path == 0:
                holder = (z * SIDE + (y + SIDE - d) % SIDE) * 2 + c
            else:
                holder = ((z + SIDE - d) % SIDE * SIDE + y) * 2 + c
            base = holder * (2 * MSG) + path * MSG
            k = path * SIDE + d
            for s in range(MSG):
                other, chip = s // (SIDE * SLOTS), s // SLOTS % SIDE
                away = ((z if path == 0 else y) + SIDE - chip) % SIDE
                block = jnp.minimum(ids[base + s], BLOCKS_DEV - 1)
                reply[k, s] = dense[other, (path * SIDE + away) * BLOCKS_DEV + block]
            copy = pltpu.make_async_copy(reply.at[k], outs[k], out_sems.at[k])
            copy.start()
            stores.append(copy)
    for copy in stores:
        copy.wait()


def make_replies(ids, place, mine, taken):
    spec = pltpu.PrefetchScalarGridSpec(
        num_scalar_prefetch=2,
        grid=(1,),
        in_specs=[ANY] * 2,
        out_specs=[ANY] * (2 * SIDE),
        scratch_shapes=[
            pltpu.VMEM((2, 2 * DENSE, REPLY, BLOCK), F32),
            pltpu.VMEM((2 * SIDE, MSG, REPLY, BLOCK), F32),
            pltpu.SemaphoreType.DMA((2,)),
            pltpu.SemaphoreType.DMA((2 * SIDE,)),
        ],
    )
    return pl.pallas_call(
        reply_kernel,
        grid_spec=spec,
        out_shape=[jax.ShapeDtypeStruct((MSG, REPLY, BLOCK), F32)] * (2 * SIDE),
        compiler_params=params(),
        name="make_replies",
    )(ids, place, mine, taken)


def add_product(acc, row, grad, tile):
    depth = grad.shape[0]
    high, low = split(tile)
    both = dot(jnp.concatenate(split(grad), axis=0), high, NN)
    acc[row] += both[:depth] + both[depth:] + dot(grad.astype(BF16), low, NN)


def hand_out(meta, acc, outs, sems):
    rep = meta[4 * TILES_DEV]
    copies = [
        pltpu.make_async_copy(
            acc.at[pl.ds((rep + d) % N_REP * BLOCKS_DEV, BLOCKS_DEV)], out, sems.at[d]
        )
        for d, out in enumerate(outs)
    ]
    for copy in copies:
        copy.start()
    for copy in copies:
        copy.wait()


def gathered_kernel(meta, tiles, grads, *rest):
    outs, (got, acc, sems, out_sems) = rest[:N_REP], rest[N_REP:]
    step = pl.program_id(0)

    @pl.when(step == 0)
    def _():
        def fetch(i, _):
            pltpu.make_async_copy(
                grads.at[meta[TILES_DEV + i]], got.at[i // STEP, i % STEP], sems.at[i // STEP]
            ).start()
            return 0

        lax.fori_loop(0, TILES_DEV, fetch, 0)
        acc[...] = jnp.zeros_like(acc)

    pltpu.make_async_copy(grads.at[pl.ds(0, STEP)], got.at[step], sems.at[step]).wait()
    for t in range(STEP):
        add_product(acc, meta[step * STEP + t], got[step, t], tiles[t])

    @pl.when(step == pl.num_programs(0) - 1)
    def _():
        hand_out(meta, acc, outs, out_sems)


def gathered_tiles(meta, tile_values, grads):
    spec = pltpu.PrefetchScalarGridSpec(
        num_scalar_prefetch=1,
        grid=(TILES_DEV // STEP,),
        in_specs=[pl.BlockSpec((STEP, BLOCK, BLOCK), lambda i, _: (i, 0, 0)), ANY],
        out_specs=[ANY] * N_REP,
        scratch_shapes=[
            pltpu.VMEM((TILES_DEV // STEP, STEP, GATHERED, BLOCK), F32),
            pltpu.VMEM((N_REP * BLOCKS_DEV, GATHERED, BLOCK), F32),
            pltpu.SemaphoreType.DMA((TILES_DEV // STEP,)),
            pltpu.SemaphoreType.DMA((N_REP,)),
        ],
    )
    return pl.pallas_call(
        gathered_kernel,
        grid_spec=spec,
        out_shape=[jax.ShapeDtypeStruct((BLOCKS_DEV, GATHERED, BLOCK), F32)] * N_REP,
        compiler_params=params(),
        name="gathered_tiles",
    )(meta, tile_values, grads)


def replied_kernel(meta, tiles, *rest):
    replies, (out, got, acc, sems, out_sem) = rest[: 2 * SIDE], rest[2 * SIDE :]
    step = pl.program_id(0)

    @pl.when(step == 0)
    def _():
        copies = [
            pltpu.make_async_copy(ref, got.at[pl.ds(k * MSG, MSG)], sems.at[k])
            for k, ref in enumerate(replies)
        ]
        for copy in copies:
            copy.start()
        acc[...] = jnp.zeros_like(acc)
        for copy in copies:
            copy.wait()

    for t in range(STEP):
        i = step * STEP + t
        grad = jnp.concatenate(
            [got[meta[2 * TILES_DEV + i]], got[meta[3 * TILES_DEV + i]]], axis=0
        )
        add_product(acc, meta[i], grad, tiles[t])

    @pl.when(step == pl.num_programs(0) - 1)
    def _():
        copy = pltpu.make_async_copy(acc, out, out_sem)
        copy.start()
        copy.wait()


def replied_tiles(meta, tile_values, replies):
    spec = pltpu.PrefetchScalarGridSpec(
        num_scalar_prefetch=1,
        grid=(TILES_DEV // STEP,),
        in_specs=[pl.BlockSpec((STEP, BLOCK, BLOCK), lambda i, _: (i, 0, 0))] + [ANY] * (2 * SIDE),
        out_specs=ANY,
        scratch_shapes=[
            pltpu.VMEM((2 * SIDE * MSG, REPLY, BLOCK), F32),
            pltpu.VMEM((N_REP * BLOCKS_DEV, REPLIED, BLOCK), F32),
            pltpu.SemaphoreType.DMA((2 * SIDE,)),
            pltpu.SemaphoreType.DMA,
        ],
    )
    return pl.pallas_call(
        replied_kernel,
        grid_spec=spec,
        out_shape=jax.ShapeDtypeStruct((N_REP * BLOCKS_DEV, REPLIED, BLOCK), F32),
        compiler_params=params(),
        name="replied_tiles",
    )(meta, tile_values, *replies)


def finish_kernel(own, *rest):
    sums, out = rest[:-1], rest[-1]
    for b in range(PER):
        pieces = [(sums[0][b] + sums[1][b]) + (sums[2][b] + sums[3][b]), sums[4][b]]
        rows = slice(b * BLOCK, (b + 1) * BLOCK)
        out[rows, :] = own[rows, :] + jnp.concatenate(pieces, axis=0).T


def finish(own, sums):
    row = pl.BlockSpec((PER * BLOCK, FEAT), lambda i: (i, 0))
    block = lambda depth: pl.BlockSpec((PER, depth, BLOCK), lambda i: (i, 0, 0))
    return pl.pallas_call(
        finish_kernel,
        grid=(BLOCKS_DEV // PER,),
        in_specs=[row] + [block(GATHERED)] * N_REP + [block(REPLIED)],
        out_specs=row,
        out_shape=jax.ShapeDtypeStruct(own.shape, F32),
        compiler_params=params(),
        name="finish_grad_x",
    )(own, *sums)


def row_index(z, y, c):
    return (z % SIDE * SIDE + y % SIDE) * 2 + c % 2


def shift(x, dz, dy, dc=0):
    pairs = [
        (row_index(z, y, c), row_index(z + dz, y + dy, c + dc))
        for z in range(SIDE)
        for y in range(SIDE)
        for c in range(2)
    ]
    return lax.ppermute(x, "row", pairs)


def shift_rep(x, d):
    return x if d == 0 else lax.ppermute(x, "rep", [(i, (i + d) % N_REP) for i in range(N_REP)])


def local(
    features, tile_values, tile_owner, tile_local, tile_source, w_self, w_neigh, bias, cotangent
):
    rep, row = lax.axis_index("rep"), lax.axis_index("row")
    z, y, c = row // (2 * SIDE), row // 2 % SIDE, row % 2

    owner = tile_owner[:, 0]
    owner_hot = owner[:, None] == jnp.arange(N_ROW, dtype=jnp.int32)[None, :]
    same = owner[:, None] == owner[None, :]
    earlier = jnp.arange(TILES_DEV)[:, None] > jnp.arange(TILES_DEV)[None, :]
    rank = jnp.sum((same & earlier).astype(jnp.int32), axis=1)
    slot = owner * SLOTS + rank
    o_z, o_y, o_c = owner // (2 * SIDE), owner // 2 % SIDE, owner % 2
    o_core = (o_c - c) % 2
    pos_y = (o_y - y) % SIDE * MSG + (o_core * SIDE + o_z) * SLOTS + rank
    pos_z = ((o_z - z) % SIDE + SIDE) * MSG + (o_core * SIDE + o_y) * SLOTS + rank
    src_rep, src_block = tile_source // BLOCKS_DEV, tile_source % BLOCKS_DEV
    src = (rep - src_rep) % N_REP * BLOCKS_DEV + src_block
    dest = owner * BLOCKS_DEV + tile_local
    forward_meta = jnp.concatenate([src, pos_y, pos_z, dest]).astype(jnp.int32)
    backward_meta = jnp.concatenate(
        [tile_source, dest, pos_y, pos_z, rep[None]]
    ).astype(jnp.int32)
    place = jnp.stack([z, y, c]).astype(jnp.int32)

    hit = slot[None, :] == jnp.arange(N_ROW * SLOTS, dtype=jnp.int32)[:, None]
    named = jnp.sum(jnp.where(hit, (tile_local - BLOCKS_DEV)[None, :], 0), axis=1) + BLOCKS_DEV
    named = named.reshape(SIDE, SIDE, 2, SLOTS)
    both = jnp.stack([named, named[:, :, ::-1]], axis=3)
    grid = (SIDE, SIDE, 2, 2, SIDE, SLOTS)
    along_z = jnp.broadcast_to(both.transpose(1, 2, 3, 0, 4)[None], grid)
    along_y = jnp.broadcast_to(both.transpose(0, 2, 3, 1, 4)[:, None], grid)
    to_send = jnp.concatenate(
        [along_z.reshape(N_ROW, MSG), along_y.reshape(N_ROW, MSG)], axis=1
    ).astype(jnp.int32)
    ids = lax.all_to_all(to_send, "row", split_axis=0, concat_axis=0, tiled=True).reshape(-1)

    half = features.shape[0] // 2
    low, high = features[:half], features[half:]
    low_1, high_3 = shift_rep(low, 1), shift_rep(high, 3)
    high_1, low_3 = shift_rep(high, 1), shift_rep(low, 3)
    to_low, to_high, forward_meta, ids = lax.optimization_barrier(
        (low_1, high_3, forward_meta, ids)
    )
    low_2, high_2 = shift_rep(to_low, 1), shift_rep(to_high, 3)
    *got, all_sums = forward_tiles(
        forward_meta,
        tile_values,
        [features, low_1, high_1, low_2, high_2, low_3, high_3],
    )
    last_rows = lax.psum_scatter(
        all_sums.reshape(-1, FEAT), "row", scatter_dimension=0, tiled=True
    ).reshape(BLOCKS_DEV, SUMMED, FEAT)
    for path, d in ORDER:
        k = path * SIDE + d
        got[k] = shift(got[k], 0, d) if path == 0 else shift(got[k], d, 0)
    keep, give = combine(ids, place, got)
    sums = list(add_cores(keep, shift(give, 0, 0, 1)))
    for path, d in ORDER:
        k = path * SIDE + d
        sums[k] = shift(sums[k], d, 0) if path == 0 else shift(sums[k], 0, d)

    output, grad_pre, aggregated, to_all, first, second = layer(
        features, cotangent, w_self, w_neigh, bias[None, :], sums + [last_rows]
    )

    gathered = lax.all_gather(to_all, "row", axis=0, tiled=True)
    dense = [first] * SIDE + [second] * SIDE
    for path, d in ORDER:
        dense[path * SIDE + d] = shift(first, d, 0) if path == 0 else shift(second, 0, d)
    mine = jnp.concatenate(dense, axis=0)
    replies = list(make_replies(ids, place, mine, shift(mine, 0, 0, 1)))
    for path, d in ORDER:
        k = path * SIDE + d
        replies[k] = shift(replies[k], 0, -d) if path == 0 else shift(replies[k], -d, 0)
    first = ORDER[0][0] * SIDE + ORDER[0][1]
    grad_pre, replies[first] = lax.optimization_barrier((grad_pre, replies[first]))

    own, terms = weight_terms(features, aggregated, grad_pre, w_self)
    dealt = lax.all_to_all(terms, "row", split_axis=0, concat_axis=0, tiled=True)
    backward_meta, dealt = lax.optimization_barrier((backward_meta, dealt))
    slab = replied_tiles(backward_meta, tile_values, replies)
    replied = lax.psum_scatter(
        slab.reshape(-1, BLOCK), "rep", scatter_dimension=0, tiled=True
    ).reshape(BLOCKS_DEV, REPLIED, BLOCK)
    row_sum = jnp.sum(dealt, axis=0)
    by_rep = jnp.stack([shift_rep(row_sum, d) for d in range(N_REP)])
    by_rep = jnp.take(by_rep, (rep - jnp.arange(N_REP)) % N_REP, axis=0)
    total = jnp.sum(by_rep, axis=0)
    slab = list(gathered_tiles(backward_meta, tile_values, gathered))
    back = [slab[0]] + [shift_rep(slab[d], d) for d in (1, 2, 3)] + [replied]
    total, back[1] = lax.optimization_barrier((total, back[1]))
    full = lax.all_to_all(
        jnp.broadcast_to(total[None], (N_ROW,) + total.shape),
        "row",
        split_axis=0,
        concat_axis=0,
        tiled=True,
    ).reshape(2 * FEAT, HID + 128)
    scale = 1.0 / math.sqrt(features.shape[0] * N_REP * N_ROW)
    grad_self = full[:FEAT, :HID] * scale
    grad_neigh = full[FEAT:, :HID] * scale
    grad_bias = jnp.concatenate([full[0, HID:], full[4, HID:]]) * scale

    grad_x = finish(own, back)
    return (output, grad_x, grad_self, grad_neigh, grad_bias)


def solution(mesh):
    return jax.shard_map(
        local,
        mesh=mesh,
        in_specs=(
            P(("rep", "row"), None),
            P(("rep", "row"), None, None),
            P(("rep", "row"), None),
            P(("rep", "row")),
            P(("rep", "row")),
            P(),
            P(),
            P(),
            P(("rep", "row"), None),
        ),
        out_specs=(P(("rep", "row"), None), P(("rep", "row"), None), P(), P(), P()),
        check_vma=False,
    )
```

```python
import functools
import math

import jax
import jax.numpy as jnp
from jax import lax
from jax.experimental import pallas as pl
from jax.experimental.pallas import tpu as pltpu
from jax.sharding import PartitionSpec as P

SLOTS = 6
BLOCK = 128
FEAT = 128
HID = 256
BLOCKS_DEV = 16
TILES_DEV = 128
N_REP = 4
SIDE = 4
N_ROW = 32
SUMMED = 48
HALF = (BLOCK - SUMMED) // 2
MSG = 2 * SIDE * SLOTS
DENSE = SIDE * BLOCKS_DEV
GATHERED = 80
REPLIED = FEAT - GATHERED
REPLY = REPLIED // 2
ORDER = ((0, 1), (0, 2), (1, 2), (1, 1), (0, 3), (1, 3))
STEP = 32
F32 = jnp.float32
BF16 = jnp.bfloat16
VMEM_LIMIT = 56 * 1024 * 1024

NN = (((1,), (0,)), ((), ()))
NT = (((1,), (1,)), ((), ()))
TN = (((0,), (0,)), ((), ()))


def params():
    return pltpu.CompilerParams(vmem_limit_bytes=VMEM_LIMIT)


def split(x):
    high = x.astype(BF16)
    return high, (x - high.astype(F32)).astype(BF16)


def dot(a, b, dims):
    return lax.dot_general(a, b, dims, preferred_element_type=F32)


def dot3(a, b, dims):
    a_high, a_low = a
    b_high, b_low = b
    return dot(a_high, b_high, dims) + dot(a_low, b_high, dims) + dot(a_high, b_low, dims)


def whole(shape):
    return pl.BlockSpec(shape, lambda *_: (0,) * len(shape))


ANY = pl.BlockSpec(memory_space=pl.ANY)


SOURCES = 7


def fill_slab(slab, refs):
    first = 0
    for ref in refs:
        high, low = split(ref[...])
        slab[first : first + ref.shape[0], :, :FEAT] = high
        slab[first : first + ref.shape[0], :, FEAT:] = low
        first += ref.shape[0]


def forward_product(tile, source):
    rows = tile.shape[0]
    both = dot(jnp.concatenate(split(tile), axis=0), source, NN)
    return both[:rows, :FEAT] + both[rows:, :FEAT] + both[:rows, FEAT:]


def forward_kernel(meta, tiles, *rest):
    sources, outs = rest[:SOURCES], rest[SOURCES : SOURCES + 2 * SIDE + 1]
    slab, send, acc, sems = rest[SOURCES + 2 * SIDE + 1 :]
    step = pl.program_id(0)

    @pl.when(step == 0)
    def _():
        fill_slab(slab, sources)
        acc[...] = jnp.zeros_like(acc)

    for t in range(STEP):
        i = step * STEP + t
        part = forward_product(tiles[t], slab[meta[i]])
        send[meta[TILES_DEV + i]] = part[:HALF]
        send[meta[2 * TILES_DEV + i]] = part[HALF : 2 * HALF]
        acc[meta[3 * TILES_DEV + i]] += part[2 * HALF :]

    @pl.when(step == pl.num_programs(0) - 1)
    def _():
        copies = [
            pltpu.make_async_copy(send.at[pl.ds(k * MSG, MSG)], out, sems.at[k])
            for k, out in enumerate(outs[:-1])
        ]
        copies.append(pltpu.make_async_copy(acc, outs[-1], sems.at[2 * SIDE]))
        for copy in copies:
            copy.start()
        for copy in copies:
            copy.wait()


def forward_tiles(meta, tile_values, sources):
    blocks = N_ROW * BLOCKS_DEV
    sources = [x.reshape(-1, BLOCK, FEAT) for x in sources]
    spec = pltpu.PrefetchScalarGridSpec(
        num_scalar_prefetch=1,
        grid=(TILES_DEV // STEP,),
        in_specs=[pl.BlockSpec((STEP, BLOCK, BLOCK), lambda i, _: (i, 0, 0))]
        + [whole(x.shape) for x in sources],
        out_specs=[ANY] * (2 * SIDE + 1),
        scratch_shapes=[
            pltpu.VMEM((N_REP * BLOCKS_DEV, BLOCK, 2 * FEAT), BF16),
            pltpu.VMEM((2 * SIDE * MSG, HALF, FEAT), F32),
            pltpu.VMEM((blocks, SUMMED, FEAT), F32),
            pltpu.SemaphoreType.DMA((2 * SIDE + 1,)),
        ],
    )
    return pl.pallas_call(
        forward_kernel,
        grid_spec=spec,
        out_shape=[jax.ShapeDtypeStruct((MSG, HALF, FEAT), F32)] * (2 * SIDE)
        + [jax.ShapeDtypeStruct((blocks, SUMMED, FEAT), F32)],
        compiler_params=params(),
        name="forward_tiles",
    )(meta, tile_values, *sources)


def combine_kernel(ids, place, *rest):
    received, (keep, give) = rest[: 2 * SIDE], rest[2 * SIDE : 2 * SIDE + 2]
    got, acc, in_sems, sems = rest[-4:]
    z, y, c = place[0], place[1], place[2]
    rows = BLOCKS_DEV + 1
    arrivals = [
        pltpu.make_async_copy(ref, got.at[k], in_sems.at[k]) for k, ref in enumerate(received)
    ]
    for copy in arrivals:
        copy.start()
    acc[...] = jnp.zeros_like(acc)
    copies = []
    for path in range(2):
        for d in range(SIDE):
            if path == 0:
                sender = (z * SIDE + (y + SIDE - d) % SIDE) * 2 + c
            else:
                sender = ((z + SIDE - d) % SIDE * SIDE + y) * 2 + c
            base = sender * (2 * MSG) + path * MSG
            arrivals[path * SIDE + d].wait()
            for s in range(MSG):
                row = (path * 2 * SIDE + s // SLOTS) * rows + ids[base + s]
                acc[row] += got[path * SIDE + d, s]
        for d in range(SIDE):
            target = ((z if path == 0 else y) + d) % SIDE
            for other, out in enumerate((keep, give)):
                copy = pltpu.make_async_copy(
                    acc.at[pl.ds(((path * 2 + other) * SIDE + target) * rows, BLOCKS_DEV)],
                    out.at[pl.ds((path * SIDE + d) * BLOCKS_DEV, BLOCKS_DEV)],
                    sems.at[(path * 2 + other) * SIDE + d],
                )
                copy.start()
                copies.append(copy)
    for copy in copies:
        copy.wait()


def combine(ids, place, received):
    spec = pltpu.PrefetchScalarGridSpec(
        num_scalar_prefetch=2,
        grid=(1,),
        in_specs=[ANY] * (2 * SIDE),
        out_specs=[ANY] * 2,
        scratch_shapes=[
            pltpu.VMEM((2 * SIDE, MSG, HALF, FEAT), F32),
            pltpu.VMEM((4 * SIDE * (BLOCKS_DEV + 1), HALF, FEAT), F32),
            pltpu.SemaphoreType.DMA((2 * SIDE,)),
            pltpu.SemaphoreType.DMA((4 * SIDE,)),
        ],
    )
    return pl.pallas_call(
        combine_kernel,
        grid_spec=spec,
        out_shape=[jax.ShapeDtypeStruct((2 * DENSE, HALF, FEAT), F32)] * 2,
        compiler_params=params(),
        name="combine_blocks",
    )(ids, place, *received)


def add_kernel(keep, taken, *rest):
    outs, (left, right, in_sems, out_sems) = rest[: 2 * SIDE], rest[2 * SIDE :]
    loads, stores = [], []
    for k in range(2 * SIDE):
        rows = pl.ds(k * BLOCKS_DEV, BLOCKS_DEV)
        for n, (ref, buffer) in enumerate(((keep, left), (taken, right))):
            copy = pltpu.make_async_copy(ref.at[rows], buffer.at[k], in_sems.at[2 * k + n])
            copy.start()
            loads.append(copy)
    for k, out in enumerate(outs):
        loads[2 * k].wait()
        loads[2 * k + 1].wait()
        left[k] += right[k]
        copy = pltpu.make_async_copy(left.at[k], out, out_sems.at[k])
        copy.start()
        stores.append(copy)
    for copy in stores:
        copy.wait()


def add_cores(keep, taken):
    return pl.pallas_call(
        add_kernel,
        in_specs=[ANY] * 2,
        out_specs=[ANY] * (2 * SIDE),
        out_shape=[jax.ShapeDtypeStruct((BLOCKS_DEV, HALF, FEAT), F32)] * (2 * SIDE),
        scratch_shapes=[
            pltpu.VMEM((2 * SIDE, BLOCKS_DEV, HALF, FEAT), F32),
            pltpu.VMEM((2 * SIDE, BLOCKS_DEV, HALF, FEAT), F32),
            pltpu.SemaphoreType.DMA((4 * SIDE,)),
            pltpu.SemaphoreType.DMA((2 * SIDE,)),
        ],
        compiler_params=params(),
        name="add_cores",
    )(keep, taken)


PER = 4


def layer_kernel(features, cotangent, w_self, w_neigh, bias, *rest):
    sums, (output, grad_pre, aggregated, gathered, first, second) = rest[:-6], rest[-6:]
    halves = []
    for b in range(PER):
        for piece in range(2):
            refs = sums[piece * SIDE : (piece + 1) * SIDE]
            halves.append((refs[0][b] + refs[1][b]) + (refs[2][b] + refs[3][b]))
        halves.append(sums[-1][b])
    agg = jnp.concatenate(halves, axis=0)
    aggregated[...] = agg
    w_neigh_split = split(w_neigh[...])
    pre = (
        dot3(split(features[...]), split(w_self[...]), NN)
        + dot3(split(agg), w_neigh_split, NN)
        + bias[...]
    )
    sigma = jax.nn.sigmoid(pre)
    output[...] = pre * sigma
    grad = cotangent[...] * sigma * (1.0 + pre * (1.0 - sigma))
    grad_pre[...] = grad
    high, low = split(grad)
    for b in range(PER):
        rows = slice(b * BLOCK, (b + 1) * BLOCK)
        turned = dot3(w_neigh_split, (high[rows], low[rows]), NT)
        gathered[b] = turned[:GATHERED]
        first[b] = turned[GATHERED : GATHERED + REPLY]
        second[b] = turned[GATHERED + REPLY :]


def layer(features, cotangent, w_self, w_neigh, bias, sums):
    nodes = features.shape[0]
    row = lambda width: pl.BlockSpec((PER * BLOCK, width), lambda i: (i, 0))
    block = lambda depth: pl.BlockSpec((PER, depth, BLOCK), lambda i: (i, 0, 0))
    return pl.pallas_call(
        layer_kernel,
        grid=(BLOCKS_DEV // PER,),
        in_specs=[row(FEAT), row(HID), whole((FEAT, HID)), whole((FEAT, HID)), whole((1, HID))]
        + [block(HALF)] * (2 * SIDE)
        + [block(SUMMED)],
        out_specs=[row(HID), row(HID), row(FEAT), block(GATHERED), block(REPLY), block(REPLY)],
        out_shape=[
            jax.ShapeDtypeStruct((nodes, HID), F32),
            jax.ShapeDtypeStruct((nodes, HID), F32),
            jax.ShapeDtypeStruct((nodes, FEAT), F32),
            jax.ShapeDtypeStruct((BLOCKS_DEV, GATHERED, BLOCK), F32),
            jax.ShapeDtypeStruct((BLOCKS_DEV, REPLY, BLOCK), F32),
            jax.ShapeDtypeStruct((BLOCKS_DEV, REPLY, BLOCK), F32),
        ],
        compiler_params=params(),
        name="layer",
    )(features, cotangent, w_self, w_neigh, bias, *sums)


TERM_ROWS = 2 * FEAT // N_ROW


def terms_kernel(features, aggregated, grad_pre, w_self, own, terms, acc, acc_bias):
    step = pl.program_id(0)

    @pl.when(step == 0)
    def _():
        acc[...] = jnp.zeros_like(acc)
        acc_bias[...] = jnp.zeros_like(acc_bias)

    grad = grad_pre[...]
    parts = split(grad)
    own[...] = dot3(parts, split(w_self[...]), NT)
    acc[:FEAT] += dot3(split(features[...]), parts, TN)
    acc[FEAT:] += dot3(split(aggregated[...]), parts, TN)
    acc_bias[...] += jnp.sum(grad.reshape(-1, 8, HID), axis=0)

    @pl.when(step == pl.num_programs(0) - 1)
    def _():
        total = jnp.sum(acc_bias[...], axis=0, keepdims=True)
        for r in range(N_ROW):
            terms[r, :, :HID] = acc[r * TERM_ROWS : (r + 1) * TERM_ROWS]
            terms[r, :, HID:] = jnp.concatenate(
                [jnp.broadcast_to(total[:, :128], (4, 128)), jnp.broadcast_to(total[:, 128:], (4, 128))],
                axis=0,
            )


def weight_terms(features, aggregated, grad_pre, w_self):
    nodes = features.shape[0]
    row = lambda width: pl.BlockSpec((PER * BLOCK, width), lambda i: (i, 0))
    return pl.pallas_call(
        terms_kernel,
        grid=(BLOCKS_DEV // PER,),
        in_specs=[row(FEAT), row(FEAT), row(HID), whole((FEAT, HID))],
        out_specs=[row(FEAT), whole((N_ROW, TERM_ROWS, HID + 128))],
        out_shape=[
            jax.ShapeDtypeStruct((nodes, FEAT), F32),
            jax.ShapeDtypeStruct((N_ROW, TERM_ROWS, HID + 128), F32),
        ],
        scratch_shapes=[pltpu.VMEM((2 * FEAT, HID), F32), pltpu.VMEM((8, HID), F32)],
        compiler_params=params(),
        name="weight_terms",
    )(features, aggregated, grad_pre, w_self)


def reply_kernel(ids, place, mine, taken, *rest):
    outs, (dense, reply, in_sems, out_sems) = rest[: 2 * SIDE], rest[2 * SIDE :]
    z, y, c = place[0], place[1], place[2]
    loads = []
    for n, ref in enumerate((mine, taken)):
        copy = pltpu.make_async_copy(ref, dense.at[n], in_sems.at[n])
        copy.start()
        loads.append(copy)
    for copy in loads:
        copy.wait()
    stores = []
    for path in range(2):
        for d in range(SIDE):
            if path == 0:
                holder = (z * SIDE + (y + SIDE - d) % SIDE) * 2 + c
            else:
                holder = ((z + SIDE - d) % SIDE * SIDE + y) * 2 + c
            base = holder * (2 * MSG) + path * MSG
            k = path * SIDE + d
            for s in range(MSG):
                other, chip = s // (SIDE * SLOTS), s // SLOTS % SIDE
                away = ((z if path == 0 else y) + SIDE - chip) % SIDE
                block = jnp.minimum(ids[base + s], BLOCKS_DEV - 1)
                reply[k, s] = dense[other, (path * SIDE + away) * BLOCKS_DEV + block]
            copy = pltpu.make_async_copy(reply.at[k], outs[k], out_sems.at[k])
            copy.start()
            stores.append(copy)
    for copy in stores:
        copy.wait()


def make_replies(ids, place, mine, taken):
    spec = pltpu.PrefetchScalarGridSpec(
        num_scalar_prefetch=2,
        grid=(1,),
        in_specs=[ANY] * 2,
        out_specs=[ANY] * (2 * SIDE),
        scratch_shapes=[
            pltpu.VMEM((2, 2 * DENSE, REPLY, BLOCK), F32),
            pltpu.VMEM((2 * SIDE, MSG, REPLY, BLOCK), F32),
            pltpu.SemaphoreType.DMA((2,)),
            pltpu.SemaphoreType.DMA((2 * SIDE,)),
        ],
    )
    return pl.pallas_call(
        reply_kernel,
        grid_spec=spec,
        out_shape=[jax.ShapeDtypeStruct((MSG, REPLY, BLOCK), F32)] * (2 * SIDE),
        compiler_params=params(),
        name="make_replies",
    )(ids, place, mine, taken)


def add_product(acc, row, grad, tile):
    depth = grad.shape[0]
    high, low = split(tile)
    both = dot(jnp.concatenate(split(grad), axis=0), high, NN)
    acc[row] += both[:depth] + both[depth:] + dot(grad.astype(BF16), low, NN)


def hand_out(meta, acc, outs, sems):
    rep = meta[4 * TILES_DEV]
    copies = [
        pltpu.make_async_copy(
            acc.at[pl.ds((rep + d) % N_REP * BLOCKS_DEV, BLOCKS_DEV)], out, sems.at[d]
        )
        for d, out in enumerate(outs)
    ]
    for copy in copies:
        copy.start()
    for copy in copies:
        copy.wait()


def gathered_kernel(meta, tiles, grads, *rest):
    outs, (got, acc, sems, out_sems) = rest[:N_REP], rest[N_REP:]
    step = pl.program_id(0)

    @pl.when(step == 0)
    def _():
        def fetch(i, _):
            pltpu.make_async_copy(
                grads.at[meta[TILES_DEV + i]], got.at[i // STEP, i % STEP], sems.at[i // STEP]
            ).start()
            return 0

        lax.fori_loop(0, TILES_DEV, fetch, 0)
        acc[...] = jnp.zeros_like(acc)

    pltpu.make_async_copy(grads.at[pl.ds(0, STEP)], got.at[step], sems.at[step]).wait()
    for t in range(STEP):
        add_product(acc, meta[step * STEP + t], got[step, t], tiles[t])

    @pl.when(step == pl.num_programs(0) - 1)
    def _():
        hand_out(meta, acc, outs, out_sems)


def gathered_tiles(meta, tile_values, grads):
    spec = pltpu.PrefetchScalarGridSpec(
        num_scalar_prefetch=1,
        grid=(TILES_DEV // STEP,),
        in_specs=[pl.BlockSpec((STEP, BLOCK, BLOCK), lambda i, _: (i, 0, 0)), ANY],
        out_specs=[ANY] * N_REP,
        scratch_shapes=[
            pltpu.VMEM((TILES_DEV // STEP, STEP, GATHERED, BLOCK), F32),
            pltpu.VMEM((N_REP * BLOCKS_DEV, GATHERED, BLOCK), F32),
            pltpu.SemaphoreType.DMA((TILES_DEV // STEP,)),
            pltpu.SemaphoreType.DMA((N_REP,)),
        ],
    )
    return pl.pallas_call(
        gathered_kernel,
        grid_spec=spec,
        out_shape=[jax.ShapeDtypeStruct((BLOCKS_DEV, GATHERED, BLOCK), F32)] * N_REP,
        compiler_params=params(),
        name="gathered_tiles",
    )(meta, tile_values, grads)


def replied_kernel(meta, tiles, *rest):
    replies, (out, got, acc, sems, out_sem) = rest[: 2 * SIDE], rest[2 * SIDE :]
    step = pl.program_id(0)

    @pl.when(step == 0)
    def _():
        copies = [
            pltpu.make_async_copy(ref, got.at[pl.ds(k * MSG, MSG)], sems.at[k])
            for k, ref in enumerate(replies)
        ]
        for copy in copies:
            copy.start()
        acc[...] = jnp.zeros_like(acc)
        for copy in copies:
            copy.wait()

    for t in range(STEP):
        i = step * STEP + t
        grad = jnp.concatenate(
            [got[meta[2 * TILES_DEV + i]], got[meta[3 * TILES_DEV + i]]], axis=0
        )
        add_product(acc, meta[i], grad, tiles[t])

    @pl.when(step == pl.num_programs(0) - 1)
    def _():
        copy = pltpu.make_async_copy(acc, out, out_sem)
        copy.start()
        copy.wait()


def replied_tiles(meta, tile_values, replies):
    spec = pltpu.PrefetchScalarGridSpec(
        num_scalar_prefetch=1,
        grid=(TILES_DEV // STEP,),
        in_specs=[pl.BlockSpec((STEP, BLOCK, BLOCK), lambda i, _: (i, 0, 0))] + [ANY] * (2 * SIDE),
        out_specs=ANY,
        scratch_shapes=[
            pltpu.VMEM((2 * SIDE * MSG, REPLY, BLOCK), F32),
            pltpu.VMEM((N_REP * BLOCKS_DEV, REPLIED, BLOCK), F32),
            pltpu.SemaphoreType.DMA((2 * SIDE,)),
            pltpu.SemaphoreType.DMA,
        ],
    )
    return pl.pallas_call(
        replied_kernel,
        grid_spec=spec,
        out_shape=jax.ShapeDtypeStruct((N_REP * BLOCKS_DEV, REPLIED, BLOCK), F32),
        compiler_params=params(),
        name="replied_tiles",
    )(meta, tile_values, *replies)


def finish_kernel(own, *rest):
    sums, out = rest[:-1], rest[-1]
    for b in range(PER):
        pieces = [(sums[0][b] + sums[1][b]) + (sums[2][b] + sums[3][b]), sums[4][b]]
        rows = slice(b * BLOCK, (b + 1) * BLOCK)
        out[rows, :] = own[rows, :] + jnp.concatenate(pieces, axis=0).T


def finish(own, sums):
    row = pl.BlockSpec((PER * BLOCK, FEAT), lambda i: (i, 0))
    block = lambda depth: pl.BlockSpec((PER, depth, BLOCK), lambda i: (i, 0, 0))
    return pl.pallas_call(
        finish_kernel,
        grid=(BLOCKS_DEV // PER,),
        in_specs=[row] + [block(GATHERED)] * N_REP + [block(REPLIED)],
        out_specs=row,
        out_shape=jax.ShapeDtypeStruct(own.shape, F32),
        compiler_params=params(),
        name="finish_grad_x",
    )(own, *sums)


def row_index(z, y, c):
    return (z % SIDE * SIDE + y % SIDE) * 2 + c % 2


def shift(x, dz, dy, dc=0):
    pairs = [
        (row_index(z, y, c), row_index(z + dz, y + dy, c + dc))
        for z in range(SIDE)
        for y in range(SIDE)
        for c in range(2)
    ]
    return lax.ppermute(x, "row", pairs)


def shift_rep(x, d):
    return x if d == 0 else lax.ppermute(x, "rep", [(i, (i + d) % N_REP) for i in range(N_REP)])


def local(
    features, tile_values, tile_owner, tile_local, tile_source, w_self, w_neigh, bias, cotangent
):
    rep, row = lax.axis_index("rep"), lax.axis_index("row")
    z, y, c = row // (2 * SIDE), row // 2 % SIDE, row % 2

    owner = tile_owner[:, 0]
    owner_hot = owner[:, None] == jnp.arange(N_ROW, dtype=jnp.int32)[None, :]
    same = owner[:, None] == owner[None, :]
    earlier = jnp.arange(TILES_DEV)[:, None] > jnp.arange(TILES_DEV)[None, :]
    rank = jnp.sum((same & earlier).astype(jnp.int32), axis=1)
    slot = owner * SLOTS + rank
    o_z, o_y, o_c = owner // (2 * SIDE), owner // 2 % SIDE, owner % 2
    o_core = (o_c - c) % 2
    pos_y = (o_y - y) % SIDE * MSG + (o_core * SIDE + o_z) * SLOTS + rank
    pos_z = ((o_z - z) % SIDE + SIDE) * MSG + (o_core * SIDE + o_y) * SLOTS + rank
    src_rep, src_block = tile_source // BLOCKS_DEV, tile_source % BLOCKS_DEV
    src = (rep - src_rep) % N_REP * BLOCKS_DEV + src_block
    dest = owner * BLOCKS_DEV + tile_local
    forward_meta = jnp.concatenate([src, pos_y, pos_z, dest]).astype(jnp.int32)
    backward_meta = jnp.concatenate(
        [tile_source, dest, pos_y, pos_z, rep[None]]
    ).astype(jnp.int32)
    place = jnp.stack([z, y, c]).astype(jnp.int32)

    hit = slot[None, :] == jnp.arange(N_ROW * SLOTS, dtype=jnp.int32)[:, None]
    named = jnp.sum(jnp.where(hit, (tile_local - BLOCKS_DEV)[None, :], 0), axis=1) + BLOCKS_DEV
    named = named.reshape(SIDE, SIDE, 2, SLOTS)
    both = jnp.stack([named, named[:, :, ::-1]], axis=3)
    grid = (SIDE, SIDE, 2, 2, SIDE, SLOTS)
    along_z = jnp.broadcast_to(both.transpose(1, 2, 3, 0, 4)[None], grid)
    along_y = jnp.broadcast_to(both.transpose(0, 2, 3, 1, 4)[:, None], grid)
    to_send = jnp.concatenate(
        [along_z.reshape(N_ROW, MSG), along_y.reshape(N_ROW, MSG)], axis=1
    ).astype(jnp.int32)
    ids = lax.all_to_all(to_send, "row", split_axis=0, concat_axis=0, tiled=True).reshape(-1)

    half = features.shape[0] // 2
    low, high = features[:half], features[half:]
    low_1, high_3 = shift_rep(low, 1), shift_rep(high, 3)
    high_1, low_3 = shift_rep(high, 1), shift_rep(low, 3)
    to_low, to_high, forward_meta, ids = lax.optimization_barrier(
        (low_1, high_3, forward_meta, ids)
    )
    low_2, high_2 = shift_rep(to_low, 1), shift_rep(to_high, 3)
    *got, all_sums = forward_tiles(
        forward_meta,
        tile_values,
        [features, low_1, high_1, low_2, high_2, low_3, high_3],
    )
    last_rows = lax.psum_scatter(
        all_sums.reshape(-1, FEAT), "row", scatter_dimension=0, tiled=True
    ).reshape(BLOCKS_DEV, SUMMED, FEAT)
    for path, d in ORDER:
        k = path * SIDE + d
        got[k] = shift(got[k], 0, d) if path == 0 else shift(got[k], d, 0)
    keep, give = combine(ids, place, got)
    sums = list(add_cores(keep, shift(give, 0, 0, 1)))
    for path, d in ORDER:
        k = path * SIDE + d
        sums[k] = shift(sums[k], d, 0) if path == 0 else shift(sums[k], 0, d)

    output, grad_pre, aggregated, to_all, first, second = layer(
        features, cotangent, w_self, w_neigh, bias[None, :], sums + [last_rows]
    )

    gathered = lax.all_gather(to_all, "row", axis=0, tiled=True)
    dense = [first] * SIDE + [second] * SIDE
    for path, d in ORDER:
        dense[path * SIDE + d] = shift(first, d, 0) if path == 0 else shift(second, 0, d)
    mine = jnp.concatenate(dense, axis=0)
    replies = list(make_replies(ids, place, mine, shift(mine, 0, 0, 1)))
    for path, d in ORDER:
        k = path * SIDE + d
        replies[k] = shift(replies[k], 0, -d) if path == 0 else shift(replies[k], -d, 0)
    first = ORDER[0][0] * SIDE + ORDER[0][1]
    grad_pre, replies[first] = lax.optimization_barrier((grad_pre, replies[first]))

    own, terms = weight_terms(features, aggregated, grad_pre, w_self)
    dealt = lax.all_to_all(terms, "row", split_axis=0, concat_axis=0, tiled=True)
    backward_meta, dealt = lax.optimization_barrier((backward_meta, dealt))
    slab = replied_tiles(backward_meta, tile_values, replies)
    replied = lax.psum_scatter(
        slab.reshape(-1, BLOCK), "rep", scatter_dimension=0, tiled=True
    ).reshape(BLOCKS_DEV, REPLIED, BLOCK)
    row_sum = jnp.sum(dealt, axis=0)
    by_rep = jnp.stack([shift_rep(row_sum, d) for d in range(N_REP)])
    by_rep = jnp.take(by_rep, (rep - jnp.arange(N_REP)) % N_REP, axis=0)
    total = jnp.sum(by_rep, axis=0)
    gathered_meta, total = lax.optimization_barrier((backward_meta, total))
    slab = list(gathered_tiles(gathered_meta, tile_values, gathered))
    back = [slab[0]] + [shift_rep(slab[d], d) for d in (1, 2, 3)] + [replied]
    total, back[1] = lax.optimization_barrier((total, back[1]))
    full = lax.all_to_all(
        jnp.broadcast_to(total[None], (N_ROW,) + total.shape),
        "row",
        split_axis=0,
        concat_axis=0,
        tiled=True,
    ).reshape(2 * FEAT, HID + 128)
    scale = 1.0 / math.sqrt(features.shape[0] * N_REP * N_ROW)
    grad_self = full[:FEAT, :HID] * scale
    grad_neigh = full[FEAT:, :HID] * scale
    grad_bias = jnp.concatenate([full[0, HID:], full[4, HID:]]) * scale

    grad_x = finish(own, back)
    return (output, grad_x, grad_self, grad_neigh, grad_bias)


def solution(mesh):
    return jax.shard_map(
        local,
        mesh=mesh,
        in_specs=(
            P(("rep", "row"), None),
            P(("rep", "row"), None, None),
            P(("rep", "row"), None),
            P(("rep", "row")),
            P(("rep", "row")),
            P(),
            P(),
            P(),
            P(("rep", "row"), None),
        ),
        out_specs=(P(("rep", "row"), None), P(("rep", "row"), None), P(), P(), P()),
        check_vma=False,
    )
```

```python
import functools
import math

import jax
import jax.numpy as jnp
from jax import lax
from jax.experimental import pallas as pl
from jax.experimental.pallas import tpu as pltpu
from jax.sharding import PartitionSpec as P

SLOTS = 6
BLOCK = 128
FEAT = 128
HID = 256
BLOCKS_DEV = 16
TILES_DEV = 128
N_REP = 4
SIDE = 4
N_ROW = 32
SUMMED = 48
HALF = (BLOCK - SUMMED) // 2
MSG = 2 * SIDE * SLOTS
DENSE = SIDE * BLOCKS_DEV
GATHERED = 80
REPLIED = FEAT - GATHERED
REPLY = REPLIED // 2
ORDER = ((0, 1), (0, 2), (1, 2), (1, 1), (0, 3), (1, 3))
STEP = 32
F32 = jnp.float32
BF16 = jnp.bfloat16
VMEM_LIMIT = 56 * 1024 * 1024

NN = (((1,), (0,)), ((), ()))
NT = (((1,), (1,)), ((), ()))
TN = (((0,), (0,)), ((), ()))


def params():
    return pltpu.CompilerParams(vmem_limit_bytes=VMEM_LIMIT)


def split(x):
    high = x.astype(BF16)
    return high, (x - high.astype(F32)).astype(BF16)


def dot(a, b, dims):
    return lax.dot_general(a, b, dims, preferred_element_type=F32)


def dot3(a, b, dims):
    a_high, a_low = a
    b_high, b_low = b
    return dot(a_high, b_high, dims) + dot(a_low, b_high, dims) + dot(a_high, b_low, dims)


def whole(shape):
    return pl.BlockSpec(shape, lambda *_: (0,) * len(shape))


ANY = pl.BlockSpec(memory_space=pl.ANY)


SOURCES = 7


def fill_slab(slab, refs):
    first = 0
    for ref in refs:
        high, low = split(ref[...])
        slab[first : first + ref.shape[0], :, :FEAT] = high
        slab[first : first + ref.shape[0], :, FEAT:] = low
        first += ref.shape[0]


def forward_product(tile, source):
    rows = tile.shape[0]
    both = dot(jnp.concatenate(split(tile), axis=0), source, NN)
    return both[:rows, :FEAT] + both[rows:, :FEAT] + both[:rows, FEAT:]


def forward_kernel(meta, tiles, *rest):
    sources, outs = rest[:SOURCES], rest[SOURCES : SOURCES + 2 * SIDE + 1]
    slab, send, acc, sems = rest[SOURCES + 2 * SIDE + 1 :]
    step = pl.program_id(0)

    @pl.when(step == 0)
    def _():
        fill_slab(slab, sources)
        acc[...] = jnp.zeros_like(acc)

    for t in range(STEP):
        i = step * STEP + t
        part = forward_product(tiles[t], slab[meta[i]])
        send[meta[TILES_DEV + i]] = part[:HALF]
        send[meta[2 * TILES_DEV + i]] = part[HALF : 2 * HALF]
        acc[meta[3 * TILES_DEV + i]] += part[2 * HALF :]

    @pl.when(step == pl.num_programs(0) - 1)
    def _():
        copies = [
            pltpu.make_async_copy(send.at[pl.ds(k * MSG, MSG)], out, sems.at[k])
            for k, out in enumerate(outs[:-1])
        ]
        copies.append(pltpu.make_async_copy(acc, outs[-1], sems.at[2 * SIDE]))
        for copy in copies:
            copy.start()
        for copy in copies:
            copy.wait()


def forward_tiles(meta, tile_values, sources):
    blocks = N_ROW * BLOCKS_DEV
    sources = [x.reshape(-1, BLOCK, FEAT) for x in sources]
    spec = pltpu.PrefetchScalarGridSpec(
        num_scalar_prefetch=1,
        grid=(TILES_DEV // STEP,),
        in_specs=[pl.BlockSpec((STEP, BLOCK, BLOCK), lambda i, _: (i, 0, 0))]
        + [whole(x.shape) for x in sources],
        out_specs=[ANY] * (2 * SIDE + 1),
        scratch_shapes=[
            pltpu.VMEM((N_REP * BLOCKS_DEV, BLOCK, 2 * FEAT), BF16),
            pltpu.VMEM((2 * SIDE * MSG, HALF, FEAT), F32),
            pltpu.VMEM((blocks, SUMMED, FEAT), F32),
            pltpu.SemaphoreType.DMA((2 * SIDE + 1,)),
        ],
    )
    return pl.pallas_call(
        forward_kernel,
        grid_spec=spec,
        out_shape=[jax.ShapeDtypeStruct((MSG, HALF, FEAT), F32)] * (2 * SIDE)
        + [jax.ShapeDtypeStruct((blocks, SUMMED, FEAT), F32)],
        compiler_params=params(),
        name="forward_tiles",
    )(meta, tile_values, *sources)


def combine_kernel(ids, place, *rest):
    received, (keep, give) = rest[: 2 * SIDE], rest[2 * SIDE : 2 * SIDE + 2]
    got, acc, in_sems, sems = rest[-4:]
    z, y, c = place[0], place[1], place[2]
    rows = BLOCKS_DEV + 1
    arrivals = [
        pltpu.make_async_copy(ref, got.at[k], in_sems.at[k]) for k, ref in enumerate(received)
    ]
    for copy in arrivals:
        copy.start()
    acc[...] = jnp.zeros_like(acc)
    copies = []
    for path in range(2):
        for d in range(SIDE):
            if path == 0:
                sender = (z * SIDE + (y + SIDE - d) % SIDE) * 2 + c
            else:
                sender = ((z + SIDE - d) % SIDE * SIDE + y) * 2 + c
            base = sender * (2 * MSG) + path * MSG
            arrivals[path * SIDE + d].wait()
            for s in range(MSG):
                row = (path * 2 * SIDE + s // SLOTS) * rows + ids[base + s]
                acc[row] += got[path * SIDE + d, s]
        for d in range(SIDE):
            target = ((z if path == 0 else y) + d) % SIDE
            for other, out in enumerate((keep, give)):
                copy = pltpu.make_async_copy(
                    acc.at[pl.ds(((path * 2 + other) * SIDE + target) * rows, BLOCKS_DEV)],
                    out.at[pl.ds((path * SIDE + d) * BLOCKS_DEV, BLOCKS_DEV)],
                    sems.at[(path * 2 + other) * SIDE + d],
                )
                copy.start()
                copies.append(copy)
    for copy in copies:
        copy.wait()


def combine(ids, place, received):
    spec = pltpu.PrefetchScalarGridSpec(
        num_scalar_prefetch=2,
        grid=(1,),
        in_specs=[ANY] * (2 * SIDE),
        out_specs=[ANY] * 2,
        scratch_shapes=[
            pltpu.VMEM((2 * SIDE, MSG, HALF, FEAT), F32),
            pltpu.VMEM((4 * SIDE * (BLOCKS_DEV + 1), HALF, FEAT), F32),
            pltpu.SemaphoreType.DMA((2 * SIDE,)),
            pltpu.SemaphoreType.DMA((4 * SIDE,)),
        ],
    )
    return pl.pallas_call(
        combine_kernel,
        grid_spec=spec,
        out_shape=[jax.ShapeDtypeStruct((2 * DENSE, HALF, FEAT), F32)] * 2,
        compiler_params=params(),
        name="combine_blocks",
    )(ids, place, *received)


def add_kernel(keep, taken, *rest):
    outs, (left, right, in_sems, out_sems) = rest[: 2 * SIDE], rest[2 * SIDE :]
    loads, stores = [], []
    for k in range(2 * SIDE):
        rows = pl.ds(k * BLOCKS_DEV, BLOCKS_DEV)
        for n, (ref, buffer) in enumerate(((keep, left), (taken, right))):
            copy = pltpu.make_async_copy(ref.at[rows], buffer.at[k], in_sems.at[2 * k + n])
            copy.start()
            loads.append(copy)
    for k, out in enumerate(outs):
        loads[2 * k].wait()
        loads[2 * k + 1].wait()
        left[k] += right[k]
        copy = pltpu.make_async_copy(left.at[k], out, out_sems.at[k])
        copy.start()
        stores.append(copy)
    for copy in stores:
        copy.wait()


def add_cores(keep, taken):
    return pl.pallas_call(
        add_kernel,
        in_specs=[ANY] * 2,
        out_specs=[ANY] * (2 * SIDE),
        out_shape=[jax.ShapeDtypeStruct((BLOCKS_DEV, HALF, FEAT), F32)] * (2 * SIDE),
        scratch_shapes=[
            pltpu.VMEM((2 * SIDE, BLOCKS_DEV, HALF, FEAT), F32),
            pltpu.VMEM((2 * SIDE, BLOCKS_DEV, HALF, FEAT), F32),
            pltpu.SemaphoreType.DMA((4 * SIDE,)),
            pltpu.SemaphoreType.DMA((2 * SIDE,)),
        ],
        compiler_params=params(),
        name="add_cores",
    )(keep, taken)


PER = 4


def layer_kernel(features, cotangent, w_self, w_neigh, bias, *rest):
    sums, (output, grad_pre, aggregated, gathered, first, second) = rest[:-6], rest[-6:]
    halves = []
    for b in range(PER):
        for piece in range(2):
            refs = sums[piece * SIDE : (piece + 1) * SIDE]
            halves.append((refs[0][b] + refs[1][b]) + (refs[2][b] + refs[3][b]))
        halves.append(sums[-1][b])
    agg = jnp.concatenate(halves, axis=0)
    aggregated[...] = agg
    w_neigh_split = split(w_neigh[...])
    pre = (
        dot3(split(features[...]), split(w_self[...]), NN)
        + dot3(split(agg), w_neigh_split, NN)
        + bias[...]
    )
    sigma = jax.nn.sigmoid(pre)
    output[...] = pre * sigma
    grad = cotangent[...] * sigma * (1.0 + pre * (1.0 - sigma))
    grad_pre[...] = grad
    high, low = split(grad)
    for b in range(PER):
        rows = slice(b * BLOCK, (b + 1) * BLOCK)
        turned = dot3(w_neigh_split, (high[rows], low[rows]), NT)
        gathered[b] = turned[:GATHERED]
        first[b] = turned[GATHERED : GATHERED + REPLY]
        second[b] = turned[GATHERED + REPLY :]


def layer(features, cotangent, w_self, w_neigh, bias, sums):
    nodes = features.shape[0]
    row = lambda width: pl.BlockSpec((PER * BLOCK, width), lambda i: (i, 0))
    block = lambda depth: pl.BlockSpec((PER, depth, BLOCK), lambda i: (i, 0, 0))
    return pl.pallas_call(
        layer_kernel,
        grid=(BLOCKS_DEV // PER,),
        in_specs=[row(FEAT), row(HID), whole((FEAT, HID)), whole((FEAT, HID)), whole((1, HID))]
        + [block(HALF)] * (2 * SIDE)
        + [block(SUMMED)],
        out_specs=[row(HID), row(HID), row(FEAT), block(GATHERED), block(REPLY), block(REPLY)],
        out_shape=[
            jax.ShapeDtypeStruct((nodes, HID), F32),
            jax.ShapeDtypeStruct((nodes, HID), F32),
            jax.ShapeDtypeStruct((nodes, FEAT), F32),
            jax.ShapeDtypeStruct((BLOCKS_DEV, GATHERED, BLOCK), F32),
            jax.ShapeDtypeStruct((BLOCKS_DEV, REPLY, BLOCK), F32),
            jax.ShapeDtypeStruct((BLOCKS_DEV, REPLY, BLOCK), F32),
        ],
        compiler_params=params(),
        name="layer",
    )(features, cotangent, w_self, w_neigh, bias, *sums)


TERM_ROWS = 2 * FEAT // N_ROW


def terms_kernel(features, aggregated, grad_pre, w_self, own, terms, acc, acc_bias):
    step = pl.program_id(0)

    @pl.when(step == 0)
    def _():
        acc[...] = jnp.zeros_like(acc)
        acc_bias[...] = jnp.zeros_like(acc_bias)

    grad = grad_pre[...]
    parts = split(grad)
    own[...] = dot3(parts, split(w_self[...]), NT)
    acc[:FEAT] += dot3(split(features[...]), parts, TN)
    acc[FEAT:] += dot3(split(aggregated[...]), parts, TN)
    acc_bias[...] += jnp.sum(grad.reshape(-1, 8, HID), axis=0)

    @pl.when(step == pl.num_programs(0) - 1)
    def _():
        total = jnp.sum(acc_bias[...], axis=0, keepdims=True)
        for r in range(N_ROW):
            terms[r, :, :HID] = acc[r * TERM_ROWS : (r + 1) * TERM_ROWS]
            terms[r, :, HID:] = jnp.concatenate(
                [jnp.broadcast_to(total[:, :128], (4, 128)), jnp.broadcast_to(total[:, 128:], (4, 128))],
                axis=0,
            )


def weight_terms(features, aggregated, grad_pre, w_self):
    nodes = features.shape[0]
    row = lambda width: pl.BlockSpec((PER * BLOCK, width), lambda i: (i, 0))
    return pl.pallas_call(
        terms_kernel,
        grid=(BLOCKS_DEV // PER,),
        in_specs=[row(FEAT), row(FEAT), row(HID), whole((FEAT, HID))],
        out_specs=[row(FEAT), whole((N_ROW, TERM_ROWS, HID + 128))],
        out_shape=[
            jax.ShapeDtypeStruct((nodes, FEAT), F32),
            jax.ShapeDtypeStruct((N_ROW, TERM_ROWS, HID + 128), F32),
        ],
        scratch_shapes=[pltpu.VMEM((2 * FEAT, HID), F32), pltpu.VMEM((8, HID), F32)],
        compiler_params=params(),
        name="weight_terms",
    )(features, aggregated, grad_pre, w_self)


def reply_kernel(ids, place, mine, taken, *rest):
    outs, (dense, reply, in_sems, out_sems) = rest[: 2 * SIDE], rest[2 * SIDE :]
    z, y, c = place[0], place[1], place[2]
    loads = []
    for n, ref in enumerate((mine, taken)):
        copy = pltpu.make_async_copy(ref, dense.at[n], in_sems.at[n])
        copy.start()
        loads.append(copy)
    for copy in loads:
        copy.wait()
    stores = []
    for path in range(2):
        for d in range(SIDE):
            if path == 0:
                holder = (z * SIDE + (y + SIDE - d) % SIDE) * 2 + c
            else:
                holder = ((z + SIDE - d) % SIDE * SIDE + y) * 2 + c
            base = holder * (2 * MSG) + path * MSG
            k = path * SIDE + d
            for s in range(MSG):
                other, chip = s // (SIDE * SLOTS), s // SLOTS % SIDE
                away = ((z if path == 0 else y) + SIDE - chip) % SIDE
                block = jnp.minimum(ids[base + s], BLOCKS_DEV - 1)
                reply[k, s] = dense[other, (path * SIDE + away) * BLOCKS_DEV + block]
            copy = pltpu.make_async_copy(reply.at[k], outs[k], out_sems.at[k])
            copy.start()
            stores.append(copy)
    for copy in stores:
        copy.wait()


def make_replies(ids, place, mine, taken):
    spec = pltpu.PrefetchScalarGridSpec(
        num_scalar_prefetch=2,
        grid=(1,),
        in_specs=[ANY] * 2,
        out_specs=[ANY] * (2 * SIDE),
        scratch_shapes=[
            pltpu.VMEM((2, 2 * DENSE, REPLY, BLOCK), F32),
            pltpu.VMEM((2 * SIDE, MSG, REPLY, BLOCK), F32),
            pltpu.SemaphoreType.DMA((2,)),
            pltpu.SemaphoreType.DMA((2 * SIDE,)),
        ],
    )
    return pl.pallas_call(
        reply_kernel,
        grid_spec=spec,
        out_shape=[jax.ShapeDtypeStruct((MSG, REPLY, BLOCK), F32)] * (2 * SIDE),
        compiler_params=params(),
        name="make_replies",
    )(ids, place, mine, taken)


def add_product(acc, row, grad, tile):
    depth = grad.shape[0]
    high, low = split(tile)
    both = dot(jnp.concatenate(split(grad), axis=0), high, NN)
    acc[row] += both[:depth] + both[depth:] + dot(grad.astype(BF16), low, NN)


def hand_out(meta, acc, outs, sems):
    rep = meta[4 * TILES_DEV]
    copies = [
        pltpu.make_async_copy(
            acc.at[pl.ds((rep + d) % N_REP * BLOCKS_DEV, BLOCKS_DEV)], out, sems.at[d]
        )
        for d, out in enumerate(outs)
    ]
    for copy in copies:
        copy.start()
    for copy in copies:
        copy.wait()


def gathered_kernel(meta, tiles, grads, *rest):
    outs, (got, acc, sems, out_sems) = rest[:N_REP], rest[N_REP:]
    step = pl.program_id(0)

    @pl.when(step == 0)
    def _():
        def fetch(i, _):
            pltpu.make_async_copy(
                grads.at[meta[TILES_DEV + i]], got.at[i // STEP, i % STEP], sems.at[i // STEP]
            ).start()
            return 0

        lax.fori_loop(0, TILES_DEV, fetch, 0)
        acc[...] = jnp.zeros_like(acc)

    pltpu.make_async_copy(grads.at[pl.ds(0, STEP)], got.at[step], sems.at[step]).wait()
    for t in range(STEP):
        add_product(acc, meta[step * STEP + t], got[step, t], tiles[t])

    @pl.when(step == pl.num_programs(0) - 1)
    def _():
        hand_out(meta, acc, outs, out_sems)


def gathered_tiles(meta, tile_values, grads):
    spec = pltpu.PrefetchScalarGridSpec(
        num_scalar_prefetch=1,
        grid=(TILES_DEV // STEP,),
        in_specs=[pl.BlockSpec((STEP, BLOCK, BLOCK), lambda i, _: (i, 0, 0)), ANY],
        out_specs=[ANY] * N_REP,
        scratch_shapes=[
            pltpu.VMEM((TILES_DEV // STEP, STEP, GATHERED, BLOCK), F32),
            pltpu.VMEM((N_REP * BLOCKS_DEV, GATHERED, BLOCK), F32),
            pltpu.SemaphoreType.DMA((TILES_DEV // STEP,)),
            pltpu.SemaphoreType.DMA((N_REP,)),
        ],
    )
    return pl.pallas_call(
        gathered_kernel,
        grid_spec=spec,
        out_shape=[jax.ShapeDtypeStruct((BLOCKS_DEV, GATHERED, BLOCK), F32)] * N_REP,
        compiler_params=params(),
        name="gathered_tiles",
    )(meta, tile_values, grads)


def replied_kernel(meta, tiles, *rest):
    replies, (out, got, acc, sems, out_sem) = rest[: 2 * SIDE], rest[2 * SIDE :]
    step = pl.program_id(0)

    @pl.when(step == 0)
    def _():
        copies = [
            pltpu.make_async_copy(ref, got.at[pl.ds(k * MSG, MSG)], sems.at[k])
            for k, ref in enumerate(replies)
        ]
        for copy in copies:
            copy.start()
        acc[...] = jnp.zeros_like(acc)
        for copy in copies:
            copy.wait()

    for t in range(STEP):
        i = step * STEP + t
        grad = jnp.concatenate(
            [got[meta[2 * TILES_DEV + i]], got[meta[3 * TILES_DEV + i]]], axis=0
        )
        add_product(acc, meta[i], grad, tiles[t])

    @pl.when(step == pl.num_programs(0) - 1)
    def _():
        copy = pltpu.make_async_copy(acc, out, out_sem)
        copy.start()
        copy.wait()


def replied_tiles(meta, tile_values, replies):
    spec = pltpu.PrefetchScalarGridSpec(
        num_scalar_prefetch=1,
        grid=(TILES_DEV // STEP,),
        in_specs=[pl.BlockSpec((STEP, BLOCK, BLOCK), lambda i, _: (i, 0, 0))] + [ANY] * (2 * SIDE),
        out_specs=ANY,
        scratch_shapes=[
            pltpu.VMEM((2 * SIDE * MSG, REPLY, BLOCK), F32),
            pltpu.VMEM((N_REP * BLOCKS_DEV, REPLIED, BLOCK), F32),
            pltpu.SemaphoreType.DMA((2 * SIDE,)),
            pltpu.SemaphoreType.DMA,
        ],
    )
    return pl.pallas_call(
        replied_kernel,
        grid_spec=spec,
        out_shape=jax.ShapeDtypeStruct((N_REP * BLOCKS_DEV, REPLIED, BLOCK), F32),
        compiler_params=params(),
        name="replied_tiles",
    )(meta, tile_values, *replies)


LAST_PER = 8


def finish_kernel(own, *rest):
    sums, out = rest[:-1], rest[-1]
    for b in range(LAST_PER):
        pieces = [(sums[0][b] + sums[1][b]) + (sums[2][b] + sums[3][b]), sums[4][b]]
        rows = slice(b * BLOCK, (b + 1) * BLOCK)
        out[rows, :] = own[rows, :] + jnp.concatenate(pieces, axis=0).T


def finish(own, sums):
    row = pl.BlockSpec((LAST_PER * BLOCK, FEAT), lambda i: (i, 0))
    block = lambda depth: pl.BlockSpec((LAST_PER, depth, BLOCK), lambda i: (i, 0, 0))
    return pl.pallas_call(
        finish_kernel,
        grid=(BLOCKS_DEV // LAST_PER,),
        in_specs=[row] + [block(GATHERED)] * N_REP + [block(REPLIED)],
        out_specs=row,
        out_shape=jax.ShapeDtypeStruct(own.shape, F32),
        compiler_params=params(),
        name="finish_grad_x",
    )(own, *sums)


def row_index(z, y, c):
    return (z % SIDE * SIDE + y % SIDE) * 2 + c % 2


def shift(x, dz, dy, dc=0):
    pairs = [
        (row_index(z, y, c), row_index(z + dz, y + dy, c + dc))
        for z in range(SIDE)
        for y in range(SIDE)
        for c in range(2)
    ]
    return lax.ppermute(x, "row", pairs)


def shift_rep(x, d):
    return x if d == 0 else lax.ppermute(x, "rep", [(i, (i + d) % N_REP) for i in range(N_REP)])


def local(
    features, tile_values, tile_owner, tile_local, tile_source, w_self, w_neigh, bias, cotangent
):
    rep, row = lax.axis_index("rep"), lax.axis_index("row")
    z, y, c = row // (2 * SIDE), row // 2 % SIDE, row % 2

    owner = tile_owner[:, 0]
    owner_hot = owner[:, None] == jnp.arange(N_ROW, dtype=jnp.int32)[None, :]
    same = owner[:, None] == owner[None, :]
    earlier = jnp.arange(TILES_DEV)[:, None] > jnp.arange(TILES_DEV)[None, :]
    rank = jnp.sum((same & earlier).astype(jnp.int32), axis=1)
    slot = owner * SLOTS + rank
    o_z, o_y, o_c = owner // (2 * SIDE), owner // 2 % SIDE, owner % 2
    o_core = (o_c - c) % 2
    pos_y = (o_y - y) % SIDE * MSG + (o_core * SIDE + o_z) * SLOTS + rank
    pos_z = ((o_z - z) % SIDE + SIDE) * MSG + (o_core * SIDE + o_y) * SLOTS + rank
    src_rep, src_block = tile_source // BLOCKS_DEV, tile_source % BLOCKS_DEV
    src = (rep - src_rep) % N_REP * BLOCKS_DEV + src_block
    dest = owner * BLOCKS_DEV + tile_local
    forward_meta = jnp.concatenate([src, pos_y, pos_z, dest]).astype(jnp.int32)
    backward_meta = jnp.concatenate(
        [tile_source, dest, pos_y, pos_z, rep[None]]
    ).astype(jnp.int32)
    place = jnp.stack([z, y, c]).astype(jnp.int32)

    hit = slot[None, :] == jnp.arange(N_ROW * SLOTS, dtype=jnp.int32)[:, None]
    named = jnp.sum(jnp.where(hit, (tile_local - BLOCKS_DEV)[None, :], 0), axis=1) + BLOCKS_DEV
    named = named.reshape(SIDE, SIDE, 2, SLOTS)
    both = jnp.stack([named, named[:, :, ::-1]], axis=3)
    grid = (SIDE, SIDE, 2, 2, SIDE, SLOTS)
    along_z = jnp.broadcast_to(both.transpose(1, 2, 3, 0, 4)[None], grid)
    along_y = jnp.broadcast_to(both.transpose(0, 2, 3, 1, 4)[:, None], grid)
    to_send = jnp.concatenate(
        [along_z.reshape(N_ROW, MSG), along_y.reshape(N_ROW, MSG)], axis=1
    ).astype(jnp.int32)
    ids = lax.all_to_all(to_send, "row", split_axis=0, concat_axis=0, tiled=True).reshape(-1)

    half = features.shape[0] // 2
    low, high = features[:half], features[half:]
    low_1, high_3 = shift_rep(low, 1), shift_rep(high, 3)
    high_1, low_3 = shift_rep(high, 1), shift_rep(low, 3)
    to_low, to_high, forward_meta, ids = lax.optimization_barrier(
        (low_1, high_3, forward_meta, ids)
    )
    low_2, high_2 = shift_rep(to_low, 1), shift_rep(to_high, 3)
    *got, all_sums = forward_tiles(
        forward_meta,
        tile_values,
        [features, low_1, high_1, low_2, high_2, low_3, high_3],
    )
    last_rows = lax.psum_scatter(
        all_sums.reshape(-1, FEAT), "row", scatter_dimension=0, tiled=True
    ).reshape(BLOCKS_DEV, SUMMED, FEAT)
    for path, d in ORDER:
        k = path * SIDE + d
        got[k] = shift(got[k], 0, d) if path == 0 else shift(got[k], d, 0)
    keep, give = combine(ids, place, got)
    sums = list(add_cores(keep, shift(give, 0, 0, 1)))
    for path, d in ORDER:
        k = path * SIDE + d
        sums[k] = shift(sums[k], d, 0) if path == 0 else shift(sums[k], 0, d)

    output, grad_pre, aggregated, to_all, first, second = layer(
        features, cotangent, w_self, w_neigh, bias[None, :], sums + [last_rows]
    )

    gathered = lax.all_gather(to_all, "row", axis=0, tiled=True)
    dense = [first] * SIDE + [second] * SIDE
    for path, d in ORDER:
        dense[path * SIDE + d] = shift(first, d, 0) if path == 0 else shift(second, 0, d)
    mine = jnp.concatenate(dense, axis=0)
    replies = list(make_replies(ids, place, mine, shift(mine, 0, 0, 1)))
    for path, d in ORDER:
        k = path * SIDE + d
        replies[k] = shift(replies[k], 0, -d) if path == 0 else shift(replies[k], -d, 0)
    first = ORDER[0][0] * SIDE + ORDER[0][1]
    grad_pre, replies[first] = lax.optimization_barrier((grad_pre, replies[first]))

    own, terms = weight_terms(features, aggregated, grad_pre, w_self)
    dealt = lax.all_to_all(terms, "row", split_axis=0, concat_axis=0, tiled=True)
    backward_meta, dealt = lax.optimization_barrier((backward_meta, dealt))
    slab = replied_tiles(backward_meta, tile_values, replies)
    replied = lax.psum_scatter(
        slab.reshape(-1, BLOCK), "rep", scatter_dimension=0, tiled=True
    ).reshape(BLOCKS_DEV, REPLIED, BLOCK)
    row_sum = jnp.sum(dealt, axis=0)
    by_rep = jnp.stack([shift_rep(row_sum, d) for d in range(N_REP)])
    by_rep = jnp.take(by_rep, (rep - jnp.arange(N_REP)) % N_REP, axis=0)
    total = jnp.sum(by_rep, axis=0)
    gathered_meta, total = lax.optimization_barrier((backward_meta, total))
    slab = list(gathered_tiles(gathered_meta, tile_values, gathered))
    back = [slab[0]] + [shift_rep(slab[d], d) for d in (1, 2, 3)] + [replied]
    total, back[1] = lax.optimization_barrier((total, back[1]))
    full = lax.all_to_all(
        jnp.broadcast_to(total[None], (N_ROW,) + total.shape),
        "row",
        split_axis=0,
        concat_axis=0,
        tiled=True,
    ).reshape(2 * FEAT, HID + 128)
    scale = 1.0 / math.sqrt(features.shape[0] * N_REP * N_ROW)
    grad_self = full[:FEAT, :HID] * scale
    grad_neigh = full[FEAT:, :HID] * scale
    grad_bias = jnp.concatenate([full[0, HID:], full[4, HID:]]) * scale

    grad_x = finish(own, back)
    return (output, grad_x, grad_self, grad_neigh, grad_bias)


def solution(mesh):
    return jax.shard_map(
        local,
        mesh=mesh,
        in_specs=(
            P(("rep", "row"), None),
            P(("rep", "row"), None, None),
            P(("rep", "row"), None),
            P(("rep", "row")),
            P(("rep", "row")),
            P(),
            P(),
            P(),
            P(("rep", "row"), None),
        ),
        out_specs=(P(("rep", "row"), None), P(("rep", "row"), None), P(), P(), P()),
        check_vma=False,
    )
```
